32 devices in a mesh: rep: 4 (over y, x), tp: 8 (over z, core).
Axes of the slice: x: 2, y: 2, z: 4, core: 2. Of those that a mesh axis runs over, the one named last changes fastest.
Arguments:
- embeds: bfloat16 [3136, 5120], P('rep', 'tp'), parts along dimension 0, may hold values from -6 to 6
- remask: int32 [3136], P('rep'), parts along dimension 0, may hold values 0 or 1
- lengths: int32 [16], P('rep'), parts along dimension 0, may hold values from 49 to 196, as said below
- mask_vec: bfloat16 [5120], P('tp'), may hold values from -6 to 6
- attn_gain: bfloat16 [5120], replicated, may hold values from 0.25 to 1.75
- w_query: bfloat16 [5120, 4096], P(None, 'tp'), may hold values from -0.078125 to 0.078125
- q_bias: bfloat16 [4096], P('tp'), may hold values from -200 to 200
- w_key: bfloat16 [5120, 1024], P(None, 'tp'), may hold values from -0.078125 to 0.078125
- w_value: bfloat16 [5120, 1024], P(None, 'tp'), may hold values from -0.078125 to 0.078125
- v_bias: bfloat16 [1024], P('tp'), may hold values from -3 to 3
- w_out: bfloat16 [4096, 5120], P('tp'), may hold values from -0.125 to 0.125
- head_gain: bfloat16 [5120], replicated, may hold values from 0.25 to 1.75
- w_head: bfloat16 [5120, 512], P(None, 'tp'), may hold values from -20 to 20
Outputs:
- hidden: bfloat16 [3136, 5120], P('rep', 'tp'), parts along dimension 0
- logprob: float32 [3136, 512], P('rep', 'tp'), parts along dimension 0
The draws below stay inside these ranges and needn't reach their ends.
There are 4 independent parts, one for each index of `rep`. The reference program is written for one: setup_inputs(seed, part) draws one part's arguments, and reference() takes and returns one part's arrays. A program takes and returns all parts, laid end to end along the dimension named above; an argument that names none is the same for every part. Nothing has to cross between parts.
Inputs may be any that keep to these rules, and one draw needn't show every extreme that they name: `lengths`: every request has at least 49 tokens, and one request of each part has exactly 196.
All inputs are finite; a program needn't handle non-finite values.
Results may differ from the reference program's by a relative error of at most 0.018.
The reference program's roundings to bfloat16 on the way (of `masked`, `normed`, `attn_prob`, `context` and `normed_head`) count: a program that leaves them out, or rounds other values in their place, can miss the bound.
Values may be sent and summed in bfloat16 or wider, within the bound.
No kernel may reach another device: no remote copies, remote signals or barrier semaphores. Data moves between devices by JAX's collectives and lax.ppermute only.
A program may use at most 128 MiB of HBM per device.

```python
import jax
import jax.numpy as jnp
from jax import lax

D = 5120
HEADS = 32
KVH = 8
HS = 128
VOCAB = 512
L = 196
REQS = 4
TOKENS = 784


def draw_lengths(key, part):
    first_key = jax.random.fold_in(key, 11)
    second_key = jax.random.fold_in(key, 12)
    drawn = jax.random.randint(first_key, (REQS,), L // 4, L + 1)
    chosen = jax.random.randint(second_key, (), 0, REQS)
    return jnp.where(jnp.arange(REQS) == chosen, L, drawn).astype(jnp.int32)


def draw_q_bias(key, part):
    base = jnp.clip(jax.random.normal(jax.random.fold_in(key, 21), (HEADS * HS,), jnp.float32), -4.0, 4.0)
    return (0.5 * base).astype(jnp.bfloat16)


def draw_w_head(key, part):
    base = jnp.clip(jax.random.normal(jax.random.fold_in(key, 31), (D, VOCAB), jnp.float32), -4.0, 4.0)
    return (base * (3.0 / D ** 0.5)).astype(jnp.bfloat16)


def touch_ends(entries, own_key, smallest, largest):
    extent = entries.shape
    spot = [jax.random.randint(jax.random.fold_in(own_key, axis), (), 0, extent[axis]) for axis in range(len(extent))]
    entries = entries.at[tuple(spot)].set(smallest)
    longest = extent.index(max(extent))
    spot[longest] = (spot[longest] + 1) % extent[longest]
    return entries.at[tuple(spot)].set(largest)


def with_spikes(values, stream_key, source, target, blocks, factor):
    def block_of(dim):
        return (jnp.arange(values.shape[dim]) // (values.shape[dim] // blocks)).reshape((-1,) + (1,) * (values.ndim - 1 - dim))

    one_side = jax.random.permutation(stream_key, blocks)[block_of(target)]
    other_side = (block_of(target) + blocks // 2) % blocks
    return jnp.where((block_of(source) == one_side) | (block_of(source) == other_side), factor * values, values)


def shard_levels(rng, extent, pieces, low, high):
    def one(axis_at, parts):
        draws = jax.random.uniform(jax.random.fold_in(jax.random.fold_in(rng, 6), axis_at), (parts,), jnp.float32, low / len(pieces), high / len(pieces))
        return jnp.repeat(jnp.exp(draws), extent[axis_at] // parts).reshape((-1,) + (1,) * (len(extent) - axis_at - 1))

    factor_of = one(*pieces[0])
    for cut in pieces[1:]:
        factor_of = factor_of * one(*cut)
    return factor_of


def normal_values(rng, extent, scale, most, pieces=(), kind=jnp.bfloat16):
    values = scale * jax.random.normal(rng, extent, jnp.float32)
    if pieces:
        values = values * shard_levels(rng, extent, pieces, -0.22, 0.18)
    return jnp.clip(values, -most, most).astype(kind)


def bell_draw_with(own_key, extent, spread, limit, pieces, heavy, kind=jnp.bfloat16):
    values = spread * jax.random.normal(own_key, extent, jnp.float32)
    if pieces:
        values = values * shard_levels(own_key, extent, pieces, -0.22, 0.18)
    return jnp.clip(with_spikes(values, jax.random.fold_in(own_key, 3), *heavy), -limit, limit).astype(kind)


def setup_inputs(seed: int = 0, part: int = 0) -> dict:
    seeds = jax.random.split(jax.random.key(seed), 14)
    own_keys = jax.random.split(jax.random.fold_in(seeds[13], part), 14)
    embeds = normal_values(own_keys[0], (TOKENS, D), 1.0, 6.0, ((1, 8),))
    remask = touch_ends((jax.random.randint(own_keys[1], (TOKENS,), 0, 2) < 1).astype(jnp.int32), jax.random.fold_in(own_keys[1], 1), 0, 1)
    lengths = draw_lengths(jax.random.fold_in(jax.random.fold_in(seeds[13], part), 71), part)
    mask_vec = normal_values(seeds[3], (D,), 1.0, 6.0, ((0, 8),))
    attn_gain = jnp.clip(1.0 + 0.15 * jax.random.normal(seeds[4], (D,), jnp.float32), 0.25, 1.75).astype(jnp.bfloat16)
    w_query = normal_values(seeds[5], (D, HEADS * HS), D ** -0.5, 0.078125, ((1, 8),))
    q_bias = draw_q_bias(jax.random.fold_in(seeds[13], 71), part)
    w_key = normal_values(seeds[7], (D, KVH * HS), D ** -0.5, 0.078125, ((1, 8),))
    w_value = normal_values(seeds[8], (D, KVH * HS), D ** -0.5, 0.078125, ((1, 8),))
    v_bias = normal_values(seeds[9], (KVH * HS,), 0.5, 3.0, ((0, 8),))
    w_out = bell_draw_with(seeds[10], (HEADS * HS, D), (HEADS * HS) ** -0.5, 0.125, ((0, 8),), (0, 1, 8, 2.0))
    head_gain = jnp.clip(1.0 + 0.15 * jax.random.normal(seeds[11], (D,), jnp.float32), 0.25, 1.75).astype(jnp.bfloat16)
    w_head = draw_w_head(jax.random.fold_in(seeds[13], 71), part)
    return {"embeds": embeds, "remask": remask, "lengths": lengths, "mask_vec": mask_vec, "attn_gain": attn_gain, "w_query": w_query, "q_bias": q_bias, "w_key": w_key, "w_value": w_value, "v_bias": v_bias, "w_out": w_out, "head_gain": head_gain, "w_head": w_head}


EPS = 1e-06

def rms_norm(matrix, gain):
    wide = matrix.astype(jnp.float32)
    inverse = lax.rsqrt(lax.optimization_barrier(jnp.mean(wide * wide, axis=-1, keepdims=True)) + EPS)
    return (wide * inverse * gain.astype(jnp.float32)).astype(jnp.bfloat16)

def reference(embeds, remask, lengths, mask_vec, attn_gain, w_query, q_bias, w_key, w_value, v_bias, w_out, head_gain, w_head):
    masked = jnp.where(remask[:, None] == 1, mask_vec[None, :], embeds)
    normed = rms_norm(masked, attn_gain)
    queries = (jnp.dot(normed, w_query, preferred_element_type=jnp.float32) + q_bias.astype(jnp.float32)).astype(jnp.bfloat16)
    key_rows = jnp.dot(normed, w_key, preferred_element_type=jnp.float32).astype(jnp.bfloat16)
    value_rows = (jnp.dot(normed, w_value, preferred_element_type=jnp.float32) + v_bias.astype(jnp.float32)).astype(jnp.bfloat16)
    group = HEADS // KVH
    q_four = queries.reshape(REQS, L, HEADS, HS).astype(jnp.float32)
    k_four = jnp.repeat(key_rows.reshape(REQS, L, KVH, HS), group, axis=2).astype(jnp.float32)
    v_four = jnp.repeat(value_rows.reshape(REQS, L, KVH, HS), group, axis=2).astype(jnp.float32)
    scores = jnp.einsum('rqhd,rkhd->rhqk', q_four, k_four) * HS ** (-0.5)
    valid = jnp.arange(L, dtype=jnp.int32)[None, :] < lengths[:, None]
    scores = jnp.where(valid[:, None, None, :], scores, jnp.float32(-1e+30))
    peak = lax.optimization_barrier(jnp.max(scores, axis=-1, keepdims=True))
    expo = jnp.exp(scores - peak)
    attn_prob = (expo / lax.optimization_barrier(jnp.sum(expo, axis=-1, keepdims=True))).astype(jnp.bfloat16)
    context = jnp.einsum('rhqk,rkhd->rqhd', attn_prob.astype(jnp.float32), v_four).astype(jnp.bfloat16)
    context = context.reshape(TOKENS, HEADS * HS)
    summed = jnp.dot(context, w_out, preferred_element_type=jnp.float32)
    hidden = (masked.astype(jnp.float32) + summed).astype(jnp.bfloat16)
    normed_head = rms_norm(hidden, head_gain)
    logits = jnp.dot(normed_head, w_head, preferred_element_type=jnp.float32)
    top = lax.optimization_barrier(jnp.max(logits, axis=-1, keepdims=True))
    log_total = top + jnp.log(lax.optimization_barrier(jnp.sum(jnp.exp(logits - top), axis=-1, keepdims=True)))
    return (hidden, logits - log_total)
```

```python
import functools

import jax
import jax.numpy as jnp
from jax import lax
from jax.experimental import pallas as pl
from jax.experimental.pallas import tpu as pltpu
from jax.sharding import PartitionSpec as P

KVH = 8
HS = 128
L = 196
CORES = 2
CHIPS = 4
EXTRA = 8


EPS = 1e-06
NT = (((1,), (1,)), ((), ()))


def swapped(value, axis, apart):
    mask = 2**apart
    pairs = [(source, source ^ mask) for source in range(lax.axis_size(axis))]
    return lax.ppermute(value, axis, pairs)


def combined_all(x, axis, combine):
    everything = jax.tree.map(lambda part: lax.all_gather(part, axis), x)
    initial = jax.tree.map(lambda part: part[0], everything)

    def lap(k, so_far):
        return combine(so_far, jax.tree.map(lambda part: part[k], everything))

    return lax.fori_loop(1, lax.axis_size(axis), lap, initial)


def rms_norm(matrix, gain):
    wide = matrix.astype(jnp.float32)
    inverse = lax.rsqrt(jnp.mean(wide * wide, axis=-1, keepdims=True) + EPS)
    return (wide * inverse * gain.astype(jnp.float32)).astype(jnp.bfloat16)


def combine_pair(first_pair, second_pair):
    top = jnp.maximum(first_pair[0], second_pair[0])
    total = first_pair[1] * jnp.exp(first_pair[0] - top) + second_pair[1] * jnp.exp(
        second_pair[0] - top
    )
    return (top, total)


def between_chips(pairs):
    return [(CORES * a + c, CORES * b + c) for a, b in pairs for c in range(CORES)]


PARTNER = between_chips([(0, 1), (1, 0), (2, 3), (3, 2)])
MIDDLE = between_chips([(1, 2), (2, 1)])
OUTWARD = between_chips([(2, 3), (1, 0)])
INWARD = between_chips([(3, 2), (0, 1)])


def permuted(value, pairs):
    return lax.ppermute(value, "tp", pairs)


def gathered_shards(own):
    partner = permuted(own, PARTNER)
    middle = permuted(own, MIDDLE)
    far_middle = permuted(partner, MIDDLE)
    near = middle + permuted(middle, OUTWARD)
    far = far_middle + permuted(far_middle, OUTWARD)
    mine = [own, partner, near, far]
    return mine + [swapped(shard, "tp", 0) for shard in mine]


def attend_kernel(heads, order, length, *refs):
    shards, (gain, w_q, w_kv, q_bias, v_bias, w_out, keep, send, context) = refs[:8], refs[8:]
    width = shards[0].shape[1]
    features = width * 8
    total = None
    for shard in shards:
        wide = shard[...].astype(jnp.float32)
        part = jnp.sum(wide * wide, axis=1, keepdims=True)
        total = part if total is None else total + part
    inverse = lax.rsqrt(total / features + EPS)
    q_sum = kv_sum = None
    for k, shard in enumerate(shards):
        block = order[k]
        rows = pl.ds(pl.multiple_of(block * width, width), width)
        scaled = shard[...].astype(jnp.float32) * inverse * gain[pl.ds(block, 1), :]
        normed = scaled.astype(jnp.bfloat16)
        q_part = jnp.dot(normed, w_q[rows, :], preferred_element_type=jnp.float32)
        kv_part = jnp.dot(normed, w_kv[rows, :], preferred_element_type=jnp.float32)
        q_sum = q_part if q_sum is None else q_sum + q_part
        kv_sum = kv_part if kv_sum is None else kv_sum + kv_part
    queries = (q_sum + q_bias[...]).astype(jnp.bfloat16)
    keys = kv_sum[:, :HS].astype(jnp.bfloat16)
    values = (kv_sum[:, HS:] + v_bias[...]).astype(jnp.bfloat16)
    count = keys.shape[0]
    valid = lax.broadcasted_iota(jnp.int32, (count, count), 1) < length[0]
    for h in range(heads):
        scores = lax.dot_general(
            queries[:, h * HS : (h + 1) * HS], keys, NT, preferred_element_type=jnp.float32
        ) * HS ** (-0.5)
        scores = jnp.where(valid, scores, jnp.float32(-1e30))
        expo = jnp.exp(scores - jnp.max(scores, axis=1, keepdims=True))
        prob = (expo / jnp.sum(expo, axis=1, keepdims=True)).astype(jnp.bfloat16)
        context[:, h * HS : (h + 1) * HS] = jnp.dot(
            prob, values, preferred_element_type=jnp.float32
        ).astype(jnp.bfloat16)
    for k in range(8):
        columns = pl.ds(pl.multiple_of(order[k] * width, width), width)
        part = jnp.dot(context[...], w_out[:, columns], preferred_element_type=jnp.float32)
        target = keep if k < 4 else send
        target[k % 4] = part.astype(jnp.bfloat16)


def head_kernel(kept, other, partner, middle, masked, gain, w_rows, hidden, keep, send):
    wide = lambda ref: ref[...].astype(jnp.float32)
    summed = (wide(kept) + wide(other)) + (wide(partner) + wide(middle))
    rounded = (wide(masked) + summed).astype(jnp.bfloat16)
    hidden[...] = rounded
    value = rounded.astype(jnp.float32)
    scaled = (value * gain[...]).astype(jnp.bfloat16)
    logits = lax.dot_general(w_rows[...], scaled, NT, preferred_element_type=jnp.float32)
    ones = jnp.ones((EXTRA, value.shape[1]), jnp.float32)
    squares = lax.dot_general(
        ones, value * value, NT, preferred_element_type=jnp.float32, precision=lax.Precision.HIGHEST
    )
    entries = w_rows.shape[0] // 8
    for place, k in enumerate((0, 4, 2, 6)):
        for target, block in ((keep, k), (send, k + 1)):
            target[place, 0:entries] = logits[block * entries : (block + 1) * entries]
            target[place, entries : entries + EXTRA] = squares


def whole(space=pltpu.VMEM):
    return pl.BlockSpec(memory_space=space)


def exchanged_head(w_head, index):
    turned = w_head.T
    entries = turned.shape[0]
    width = turned.shape[1] // 8
    parts = lax.axis_size("rep")
    if entries % (16 * parts) == 0:
        share = entries // parts
        turned = lax.dynamic_slice_in_dim(turned, lax.axis_index("rep") * share, share, axis=0)
    else:
        parts, share = 1, entries
    blocks = [
        lax.dynamic_slice_in_dim(turned, jnp.bitwise_xor(index, k) * width, width, axis=1)
        for k in range(8)
    ]
    blocks = jnp.stack(blocks)
    for level in range(3):
        bit = 1 << level
        stay = [k for k in range(8) if not k & bit]
        move = [k for k in range(8) if k & bit]
        got = swapped(jnp.stack([blocks[k] for k in move]), "tp", level)
        merged = [None] * 8
        for place, k in enumerate(stay):
            merged[k] = blocks[k]
        for place, k in enumerate(move):
            merged[k] = got[place]
        blocks = jnp.stack(merged)
    if parts > 1:
        blocks = lax.all_gather(blocks, "rep", axis=1, tiled=True)
    return blocks.reshape(8 * entries, width)


def on_line(
    embeds,
    remask,
    lengths,
    mask_vec,
    attn_gain,
    w_query,
    q_bias,
    w_key,
    w_value,
    v_bias,
    w_out,
    head_gain,
    w_head,
):
    requests = lengths.shape[0]
    width = embeds.shape[1]
    heads = w_query.shape[1] // HS
    entries = w_head.shape[1]
    index = lax.axis_index("tp")
    chip, core = index // CORES, index % CORES
    first_half = chip < 2
    line = jnp.stack(
        [chip, jnp.bitwise_xor(chip, 1), jnp.where(first_half, 2, 1), jnp.where(first_half, 3, 0)]
    )
    order = jnp.concatenate([line * CORES + core, line * CORES + (1 - core)]).astype(jnp.int32)
    w_kv = jnp.concatenate([w_key, w_value], axis=1)
    gain = attn_gain.astype(jnp.float32).reshape(8, width)
    q_row = q_bias.astype(jnp.float32)[None, :]
    v_row = v_bias.astype(jnp.float32)[None, :]
    gain_local = lax.dynamic_slice_in_dim(head_gain, index * width, width).astype(jnp.float32)[None, :]
    w_rows = exchanged_head(w_head, index)

    attend = pl.pallas_call(
        functools.partial(attend_kernel, heads),
        out_shape=[jax.ShapeDtypeStruct((4, L, width), jnp.bfloat16)] * 2,
        in_specs=[whole(pltpu.SMEM)] * 2 + [whole()] * 14,
        out_specs=[whole()] * 2,
        scratch_shapes=[pltpu.VMEM((L, heads * HS), jnp.bfloat16)],
        compiler_params=pltpu.CompilerParams(vmem_limit_bytes=40 * 2**20),
        cost_estimate=pl.CostEstimate(
            flops=2 * L * width * 8 * (heads * HS * 2 + 2 * HS), bytes_accessed=16 * 2**20, transcendentals=heads * L * L
        ),
    )
    head = pl.pallas_call(
        head_kernel,
        out_shape=[
            jax.ShapeDtypeStruct((L, width), jnp.bfloat16),
            jax.ShapeDtypeStruct((4, entries + EXTRA, L), jnp.float32),
            jax.ShapeDtypeStruct((4, entries + EXTRA, L), jnp.float32),
        ],
        in_specs=[whole()] * 7,
        out_specs=[whole()] * 3,
        compiler_params=pltpu.CompilerParams(vmem_limit_bytes=16 * 2**20),
        cost_estimate=pl.CostEstimate(
            flops=2 * L * width * 8 * entries, bytes_accessed=3 * 2**20, transcendentals=0
        ),
    )

    add = lambda *terms: sum(term.astype(jnp.float32) for term in terms).astype(jnp.bfloat16)
    hiddens, logits_all, pairs_all = [], [], []
    for r in range(requests):
        rows = slice(r * L, (r + 1) * L)
        masked = jnp.where(remask[rows, None] == 1, mask_vec[None, :], embeds[rows])
        shards = gathered_shards(masked)
        keep, send = attend(order, lengths[r : r + 1], *shards, gain, w_query, w_kv, q_row, v_row, w_out)
        other = swapped(send, "tp", 0)
        far = add(keep[3], other[3])
        near = add(keep[2], other[2])
        far_in = permuted(far, INWARD)
        near_in = permuted(near, INWARD)
        far_middle = permuted(add(far, far_in), MIDDLE)
        near_middle = permuted(add(near, near_in), MIDDLE)
        partner = permuted(add(keep[1], other[1], far_middle), PARTNER)
        hidden, kept, sent = head(keep[0], other[0], partner, near_middle, masked, gain_local, w_rows)
        hiddens.append(hidden)
        held = kept + swapped(sent, "tp", 0)
        held = held[:2] + swapped(held[2:], "tp", 1)
        held = held[0] + swapped(held[1], "tp", 2)
        inverse = lax.rsqrt(held[entries] / (8 * width) + EPS)
        logits = held[:entries] * inverse[None, :]
        top = jnp.max(logits, axis=0)
        logits_all.append(logits)
        pairs_all.append(jnp.stack([top, jnp.sum(jnp.exp(logits - top[None, :]), axis=0)]))
    pair = jnp.concatenate(pairs_all, axis=1)
    for level in range(3):
        pair = jnp.stack(combine_pair(pair, swapped(pair, "tp", level)))
    log_total = pair[0] + jnp.log(pair[1])
    logits = jnp.concatenate(logits_all, axis=1)
    return (jnp.concatenate(hiddens, axis=0), (logits - log_total[None, :]).T)


def on_device(
    embeds,
    remask,
    lengths,
    mask_vec,
    attn_gain,
    w_query,
    q_bias,
    w_key,
    w_value,
    v_bias,
    w_out,
    head_gain,
    w_head,
):
    requests = lengths.shape[0]
    tokens_all = embeds.shape[0]
    masked_local = jnp.where(remask[:, None] == 1, mask_vec[None, :], embeds)
    gathered = lax.all_gather(masked_local, "tp", axis=1, tiled=True)
    normed = rms_norm(gathered, attn_gain)
    queries = (
        jnp.dot(normed, w_query, preferred_element_type=jnp.float32) + q_bias.astype(jnp.float32)
    ).astype(jnp.bfloat16)
    key_rows = jnp.dot(normed, w_key, preferred_element_type=jnp.float32).astype(jnp.bfloat16)
    value_rows = (
        jnp.dot(normed, w_value, preferred_element_type=jnp.float32) + v_bias.astype(jnp.float32)
    ).astype(jnp.bfloat16)
    tp_count = lax.axis_size("tp")
    span = max(1, tp_count // KVH)
    levels = span.bit_length() - 1
    my_index = lax.axis_index("tp")
    for level in range(levels):
        other_key, other_value = swapped((key_rows, value_rows), "tp", level)
        lower = jnp.bitwise_and(jnp.right_shift(my_index, level), 1) == 0
        key_rows = jnp.where(
            lower,
            jnp.concatenate([key_rows, other_key], axis=1),
            jnp.concatenate([other_key, key_rows], axis=1),
        )
        value_rows = jnp.where(
            lower,
            jnp.concatenate([value_rows, other_value], axis=1),
            jnp.concatenate([other_value, value_rows], axis=1),
        )
    heads_dev = queries.shape[1] // HS
    kv_count = key_rows.shape[1] // HS
    repeats = heads_dev // kv_count
    k_four = jnp.repeat(key_rows.reshape(requests, L, kv_count, HS), repeats, axis=2)
    v_four = jnp.repeat(value_rows.reshape(requests, L, kv_count, HS), repeats, axis=2)
    q_four = queries.reshape(requests, L, heads_dev, HS)
    scores = jnp.einsum(
        "rqhd,rkhd->rhqk", q_four, k_four, preferred_element_type=jnp.float32
    ) * HS ** (-0.5)
    valid = jnp.arange(L, dtype=jnp.int32)[None, :] < lengths[:, None]
    scores = jnp.where(valid[:, None, None, :], scores, jnp.float32(-1e30))
    peak = jnp.max(scores, axis=-1, keepdims=True)
    expo = jnp.exp(scores - peak)
    attn_prob = (expo / jnp.sum(expo, axis=-1, keepdims=True)).astype(jnp.bfloat16)
    context = jnp.einsum(
        "rhqk,rkhd->rqhd", attn_prob, v_four, preferred_element_type=jnp.float32
    ).astype(jnp.bfloat16)
    context = context.reshape(tokens_all, heads_dev * HS)
    portion = lax.psum_scatter(
        lax.dot_general(
            w_out, context, (((0,), (1,)), ((), ())), preferred_element_type=jnp.float32
        ).astype(jnp.bfloat16),
        "tp",
        scatter_dimension=0,
        tiled=True,
    ).astype(jnp.float32)
    hidden_local = (masked_local.astype(jnp.float32) + portion.T).astype(jnp.bfloat16)
    hidden_full = lax.all_gather(hidden_local, "tp", axis=1, tiled=True)
    normed_head = rms_norm(hidden_full, head_gain)
    logits = jnp.dot(normed_head, w_head, preferred_element_type=jnp.float32)
    local_top = jnp.max(logits, axis=-1)
    local_total = jnp.sum(jnp.exp(logits - local_top[:, None]), axis=-1)
    row_top, row_total = combined_all((local_top, local_total), "tp", combine_pair)
    log_total = row_top + jnp.log(row_total)
    return (hidden_local, logits - log_total[:, None])


def solution(mesh):
    placed = (
        P("rep", "tp"),
        P("rep"),
        P("rep"),
        P("tp"),
        P(),
        P(None, "tp"),
        P("tp"),
        P(None, "tp"),
        P(None, "tp"),
        P("tp"),
        P("tp", None),
        P(),
        P(None, "tp"),
    )
    on_line_fits = mesh.shape["tp"] == CORES * CHIPS and mesh.shape["tp"] == KVH
    return jax.shard_map(
        on_line if on_line_fits else on_device,
        mesh=mesh,
        in_specs=placed,
        out_specs=(P("rep", "tp"), P("rep", "tp")),
        check_vma=False,
    )
```

```python
import functools

import jax
import jax.numpy as jnp
from jax import lax
from jax.experimental import pallas as pl
from jax.experimental.pallas import tpu as pltpu
from jax.sharding import PartitionSpec as P

KVH = 8
HS = 128
L = 196
CORES = 2
CHIPS = 4
EXTRA = 16
LANES = 256
HEAD_SPREAD = True
SPLIT_OUT = True
VMEM_A = 56
STAGES = 2
VMEM_B = 56
GROUPS = [(0, 2), (2, 4)]


EPS = 1e-06
NT = (((1,), (1,)), ((), ()))


def swapped(value, axis, apart):
    mask = 2**apart
    pairs = [(source, source ^ mask) for source in range(lax.axis_size(axis))]
    return lax.ppermute(value, axis, pairs)


def combined_all(x, axis, combine):
    everything = jax.tree.map(lambda part: lax.all_gather(part, axis), x)
    initial = jax.tree.map(lambda part: part[0], everything)

    def lap(k, so_far):
        return combine(so_far, jax.tree.map(lambda part: part[k], everything))

    return lax.fori_loop(1, lax.axis_size(axis), lap, initial)


def rms_norm(matrix, gain):
    wide = matrix.astype(jnp.float32)
    inverse = lax.rsqrt(jnp.mean(wide * wide, axis=-1, keepdims=True) + EPS)
    return (wide * inverse * gain.astype(jnp.float32)).astype(jnp.bfloat16)


def combine_pair(first_pair, second_pair):
    top = jnp.maximum(first_pair[0], second_pair[0])
    total = first_pair[1] * jnp.exp(first_pair[0] - top) + second_pair[1] * jnp.exp(
        second_pair[0] - top
    )
    return (top, total)


def between_chips(pairs):
    return [(CORES * a + c, CORES * b + c) for a, b in pairs for c in range(CORES)]


PARTNER = between_chips([(0, 1), (1, 0), (2, 3), (3, 2)])
MIDDLE = between_chips([(1, 2), (2, 1)])
OUTWARD = between_chips([(2, 3), (1, 0)])
INWARD = between_chips([(3, 2), (0, 1)])


def permuted(value, pairs):
    return lax.ppermute(value, "tp", pairs)


def after(value, *earlier):
    return lax.optimization_barrier((value, earlier))[0]


def attend_kernel(heads, order, length, *refs):
    shards, (gain, w_q, w_kv, q_bias, v_bias, context, normed, q_rows, kv_rows, sems) = refs[:8], refs[8:]
    width = shards[0].shape[1]
    group, count = context.shape[:2]
    copies = []
    for k in range(8):
        rows = pl.ds(pl.multiple_of(order[k] * width, width), width)
        here = slice(k * width, (k + 1) * width)
        copies.append(
            (
                pltpu.make_async_copy(w_q.at[rows, :], q_rows.at[here, :], sems.at[0, k]),
                pltpu.make_async_copy(w_kv.at[rows, :], kv_rows.at[here, :], sems.at[1, k]),
            )
        )
        for copy in copies[-1]:
            copy.start()
    total = None
    for k in range(8):
        wide = shards[k][...].astype(jnp.float32)
        part = jnp.sum(wide * wide, axis=1, keepdims=True)
        total = part if total is None else total + part
    inverse = lax.rsqrt(total / (8 * width) + EPS)
    for k in range(8):
        scaled = shards[k][...].astype(jnp.float32) * inverse * gain[pl.ds(order[k], 1), :]
        normed[:, k * width : (k + 1) * width] = scaled.astype(jnp.bfloat16)
    q_sum = kv_sum = None
    each = 8 // STAGES
    for stage in range(STAGES):
        for k in range(stage * each, (stage + 1) * each):
            for copy in copies[k]:
                copy.wait()
        rows = slice(stage * each * width, (stage + 1) * each * width)
        q_part = jnp.dot(normed[:, rows], q_rows[rows, :], preferred_element_type=jnp.float32)
        kv_part = jnp.dot(normed[:, rows], kv_rows[rows, :], preferred_element_type=jnp.float32)
        q_sum = q_part if q_sum is None else q_sum + q_part
        kv_sum = kv_part if kv_sum is None else kv_sum + kv_part
    q_sum += q_bias[...]
    for g in range(group):
        here = slice(g * count, (g + 1) * count)
        queries = q_sum[here].astype(jnp.bfloat16)
        keys = kv_sum[here, :HS].astype(jnp.bfloat16)
        values = (kv_sum[here, HS:] + v_bias[...]).astype(jnp.bfloat16)
        valid = lax.broadcasted_iota(jnp.int32, (1, count), 1) < length[g]
        done = []
        for h in range(heads):
            scores = lax.dot_general(
                queries[:, h * HS : (h + 1) * HS], keys, NT, preferred_element_type=jnp.float32
            )
            scores = jnp.where(valid, scores, jnp.float32(-1e30))
            expo = jnp.exp((scores - jnp.max(scores, axis=1, keepdims=True)) * HS ** (-0.5))
            share = 1.0 / jnp.sum(expo, axis=1, keepdims=True)
            mixed = jnp.dot(expo.astype(jnp.bfloat16), values, preferred_element_type=jnp.float32)
            done.append((mixed * share).astype(jnp.bfloat16))
        for h in range(heads):
            context[g, :, h * HS : (h + 1) * HS] = done[h]


def out_kernel(places, own, other, w_own, w_other, *refs):
    targets, (own_rows, other_rows, own_sems, other_sems) = refs[:-4], refs[-4:]
    group, _, width = targets[0].shape
    copies = []
    for k in range(len(targets)):
        columns = pl.ds(pl.multiple_of(places[k] * width, width), width)
        copies.append(
            (
                pltpu.make_async_copy(w_own.at[:, columns], own_rows.at[k], own_sems.at[k]),
                pltpu.make_async_copy(w_other.at[:, columns], other_rows.at[k], other_sems.at[k]),
            )
        )
        for copy in copies[-1]:
            copy.start()
    for k in range(len(targets)):
        for copy in copies[k]:
            copy.wait()
        for g in range(group):
            part = jnp.dot(own[g], own_rows[k], preferred_element_type=jnp.float32)
            part += jnp.dot(other[g], other_rows[k], preferred_element_type=jnp.float32)
            targets[k][g] = part.astype(jnp.bfloat16)


def head_kernel(groups, *refs):
    chunks, refs = refs[: 4 * len(groups)], refs[4 * len(groups) :]
    gain, w_rows = refs[:2]
    hiddens, (keep, send) = refs[2:-2], refs[-2:]
    entries = w_rows.shape[0] // 8
    place = 0
    for i, group in enumerate(groups):
        kept, partner, middle, masked = chunks[4 * i : 4 * i + 4]
        for g in range(group):
            wide = lambda ref: ref[g].astype(jnp.float32)
            summed = wide(kept) + (wide(partner) + wide(middle))
            rounded = (wide(masked) + summed).astype(jnp.bfloat16)
            hiddens[i][g] = rounded
            value = rounded.astype(jnp.float32)
            scaled = (value * gain[...]).astype(jnp.bfloat16)
            logits = lax.dot_general(w_rows[...], scaled, NT, preferred_element_type=jnp.float32)
            ones = jnp.ones((EXTRA // 2, value.shape[1]), jnp.float32)
            squares = lax.dot_general(
                ones, value * value, NT, preferred_element_type=jnp.float32, precision=lax.Precision.HIGHEST
            )
            coarse = squares.astype(jnp.bfloat16)
            fine = (squares - coarse.astype(jnp.float32)).astype(jnp.bfloat16)
            both = jnp.concatenate([coarse, fine], axis=0)
            lanes = slice(place * LANES, place * LANES + value.shape[0])
            place += 1
            for row, k in enumerate((0, 4, 2, 6)):
                for target, block in ((keep, k), (send, k + 1)):
                    part = logits[block * entries : (block + 1) * entries]
                    target[row, 0:entries, lanes] = part.astype(jnp.bfloat16)
                    target[row, entries : entries + EXTRA, lanes] = both


def whole(space=pltpu.VMEM):
    return pl.BlockSpec(memory_space=space)


def head_steps(w_head, index):
    turned = w_head.T
    entries = turned.shape[0]
    width = turned.shape[1] // 8
    parts = lax.axis_size("rep")
    rep = lax.axis_index("rep")
    shared = parts & (parts - 1) == 0 and entries % (16 * parts) == 0
    if shared:
        share = entries // parts
        turned = lax.dynamic_slice_in_dim(turned, rep * share, share, axis=0)
    blocks = jnp.stack(
        [
            lax.dynamic_slice_in_dim(turned, jnp.bitwise_xor(index, k) * width, width, axis=1)
            for k in range(8)
        ]
    )
    for level in range(3):
        bit = 1 << level
        stay = [k for k in range(8) if not k & bit]
        move = [k for k in range(8) if k & bit]
        got = yield swapped(jnp.stack([blocks[k] for k in move]), "tp", level)
        merged = [None] * 8
        for place, k in enumerate(stay):
            merged[k] = blocks[k]
        for place, k in enumerate(move):
            merged[k] = got[place]
        blocks = jnp.stack(merged)
    if shared:
        for level in range(parts.bit_length() - 1):
            got = yield swapped(blocks, "rep", level)
            lower = jnp.bitwise_and(jnp.right_shift(rep, level), 1) == 0
            blocks = jnp.concatenate(
                [jnp.where(lower, blocks, got), jnp.where(lower, got, blocks)], axis=1
            )
    yield blocks.reshape(8 * entries, width)


def on_line(
    embeds,
    remask,
    lengths,
    mask_vec,
    attn_gain,
    w_query,
    q_bias,
    w_key,
    w_value,
    v_bias,
    w_out,
    head_gain,
    w_head,
):
    requests = lengths.shape[0]
    width = embeds.shape[1]
    heads = w_query.shape[1] // HS
    entries = w_head.shape[1]
    index = lax.axis_index("tp")
    chip, core = index // CORES, index % CORES
    first_half = chip < 2
    line = jnp.stack(
        [chip, jnp.bitwise_xor(chip, 1), jnp.where(first_half, 2, 1), jnp.where(first_half, 3, 0)]
    ).astype(jnp.int32)
    places = jnp.concatenate([line * CORES + core, line * CORES + (1 - core)])
    by_request = embeds.reshape(requests, L, width)
    chosen = remask.reshape(requests, L, 1) == 1
    masked, flat = [], []
    for first, end in GROUPS:
        rows = slice(first * L, end * L)
        flat.append(jnp.where(remask[rows, None] == 1, mask_vec[None, :], embeds[rows]))
        masked.append(jnp.where(chosen[first:end], mask_vec[None, None, :], by_request[first:end]))
    sizes = [end - first for first, end in GROUPS]

    def of_core(matrix, wanted):
        return jnp.concatenate(
            [
                lax.dynamic_slice_in_dim(matrix, (CORES * z + wanted) * width, width, axis=1)
                for z in range(CHIPS)
            ],
            axis=1,
        )

    w_own = of_core(w_out, core)
    w_other = swapped(of_core(w_out, 1 - core), "tp", 0)
    w_kv = jnp.concatenate([w_key, w_value], axis=1)
    gain = attn_gain.astype(jnp.float32).reshape(8, width)
    q_row = q_bias.astype(jnp.float32)[None, :]
    v_row = v_bias.astype(jnp.float32)[None, :]
    gain_local = lax.dynamic_slice_in_dim(head_gain, index * width, width).astype(jnp.float32)[None, :]

    steps = head_steps(w_head, index)
    moving = [next(steps)]

    def step_head():
        try:
            moving[0] = steps.send(moving[0])
        except StopIteration:
            pass

    def attend(i):
        first, end = GROUPS[i]
        return pl.pallas_call(
            functools.partial(attend_kernel, heads),
            out_shape=jax.ShapeDtypeStruct((sizes[i], L, heads * HS), jnp.bfloat16),
            in_specs=[whole(pltpu.SMEM)] * 2 + [whole()] * 9 + [whole(pl.ANY)] * 2 + [whole()] * 2,
            out_specs=whole(),
            scratch_shapes=[
                pltpu.VMEM((sizes[i] * L, 8 * width), jnp.bfloat16),
                pltpu.VMEM((8 * width, heads * HS), jnp.bfloat16),
                pltpu.VMEM((8 * width, 2 * HS), jnp.bfloat16),
                pltpu.SemaphoreType.DMA((2, 8)),
            ],
            compiler_params=pltpu.CompilerParams(vmem_limit_bytes=VMEM_A * 2**20),
            cost_estimate=pl.CostEstimate(
                flops=sizes[i] * 2 * L * width * 8 * (heads * HS + 2 * HS),
                bytes_accessed=sizes[i] * 12 * 2**20,
                transcendentals=sizes[i] * heads * L * L,
            ),
        )(places, lengths[first:end], *shards[i], gain, w_query, w_kv, q_row, v_row)

    def out(size, wanted, *operands):
        count = wanted.shape[0]
        return pl.pallas_call(
            out_kernel,
            out_shape=[jax.ShapeDtypeStruct((size, L, width), jnp.bfloat16)] * count,
            in_specs=[whole(pltpu.SMEM)] + [whole()] * 2 + [whole(pl.ANY)] * 2,
            out_specs=[whole()] * count,
            scratch_shapes=[
                pltpu.VMEM((count, heads * HS, width), jnp.bfloat16),
                pltpu.VMEM((count, heads * HS, width), jnp.bfloat16),
                pltpu.SemaphoreType.DMA((count,)),
                pltpu.SemaphoreType.DMA((count,)),
            ],
            compiler_params=pltpu.CompilerParams(vmem_limit_bytes=VMEM_B * 2**20),
            cost_estimate=pl.CostEstimate(
                flops=size * 2 * L * width * 2 * count * heads * HS,
                bytes_accessed=size * 4 * count * 2**20,
                transcendentals=0,
            ),
        )(wanted, *operands)

    def head(groups, chunks):
        count = sum(groups)
        return pl.pallas_call(
            functools.partial(head_kernel, groups),
            out_shape=[jax.ShapeDtypeStruct((size, L, width), jnp.bfloat16) for size in groups]
            + [jax.ShapeDtypeStruct((4, entries + EXTRA, count * LANES), jnp.bfloat16)] * 2,
            in_specs=[whole()] * (4 * len(groups) + 2),
            out_specs=[whole()] * (len(groups) + 2),
            compiler_params=pltpu.CompilerParams(vmem_limit_bytes=32 * 2**20),
            cost_estimate=pl.CostEstimate(
                flops=count * 2 * L * width * 8 * entries, bytes_accessed=count * 3 * 2**20, transcendentals=0
            ),
        )(*[value for chunk in chunks for value in chunk], gain_local, moving[0])

    add = lambda *terms: sum(term.astype(jnp.float32) for term in terms).astype(jnp.bfloat16)
    last = len(GROUPS) - 1
    own, inward, middle, partner = ({} for _ in range(4))

    def advance_middle(i, *earlier):
        value = add(own[i][2], after(inward[i], *earlier))
        middle[i] = permuted(value, MIDDLE)
        return value

    def advance_partner(i, *earlier):
        value = add(own[i][1], after(middle[i][0], *earlier))
        partner[i] = permuted(value, PARTNER)
        return value

    def add_sums(kept, got):
        total = kept.astype(jnp.float32) + got.astype(jnp.float32)
        logits, coarse, fine = jnp.split(total, [entries, entries + EXTRA // 2], axis=-2)
        squares = coarse + fine
        coarse = squares.astype(jnp.bfloat16)
        fine = (squares - coarse.astype(jnp.float32)).astype(jnp.bfloat16)
        return jnp.concatenate([logits.astype(jnp.bfloat16), coarse, fine], axis=-2)

    def both_cores(*mine):
        return [*mine, *(swapped(shard, "tp", 0) for shard in mine)]

    own = flat[0]
    partner, middle = permuted(own, PARTNER), permuted(own, MIDDLE)
    far_middle, near_out = permuted(partner, MIDDLE), permuted(middle, OUTWARD)
    if HEAD_SPREAD:
        moving[0] = after(moving[0], partner)
        step_head()
        moving[0] = after(moving[0], far_middle)
        step_head()
    far_out = permuted(far_middle, OUTWARD)
    shards = [both_cores(own, partner, middle + near_out, far_middle + far_out)]

    own = after(flat[1], far_middle)
    middle = permuted(own, MIDDLE)
    own = after(own, far_out)
    partner = permuted(own, PARTNER)
    shards[0] = after(shards[0], own)
    context = attend(0)
    other = after(swapped(context, "tp", 0), partner, moving[0])
    step_head()
    far_middle, near_out = permuted(partner, MIDDLE), permuted(after(middle, partner), OUTWARD)
    self_part, partner_part, near, far = out(sizes[0], line, context, other, w_own, w_other)
    far_out = permuted(far_middle, OUTWARD)
    shards.append(both_cores(own, partner, middle + near_out, far_middle + far_out))
    far_in = permuted(after(far, far_middle), INWARD)
    far = add(far, far_in)
    far_middle = permuted(far, MIDDLE)
    near_in = permuted(after(near, far_in), INWARD)

    shards[1] = after(shards[1], far, moving[0])
    step_head()
    context = attend(1)
    other = after(swapped(context, "tp", 0), far_middle, near_in)
    partner_part, near = add(partner_part, far_middle), add(near, near_in)
    first_parts = [self_part, permuted(partner_part, PARTNER), permuted(near, MIDDLE), masked[0]]
    other = after(other, partner_part, near)
    if SPLIT_OUT:
        (far,) = out(sizes[1], line[3:], context, other, w_own, w_other)
        far_in = permuted(far, INWARD)
        other = after(other, far)
        self_part, partner_part, near = out(sizes[1], line[:3], context, other, w_own, w_other)
    else:
        self_part, partner_part, near, far = out(sizes[1], line, context, other, w_own, w_other)
        far_in = permuted(far, INWARD)
    far_middle = permuted(add(far, after(far_in, first_parts)), MIDDLE)
    near_in = permuted(after(near, far_in), INWARD)
    while moving[0].shape != (8 * entries, width):
        step_head()
    hidden_first, kept, sent = head(sizes[:1], [after(first_parts, near)])
    from_partner = permuted(add(partner_part, far_middle), PARTNER)
    near_middle = permuted(add(near, after(near_in, far_middle)), MIDDLE)
    sent = swapped(sent, "tp", 0)
    held = add_sums(kept, sent)
    move = swapped(held[2:], "tp", 1)
    held = add_sums(held[:2], move)
    move = swapped(held[1], "tp", 2)
    from_partner = after(from_partner, move)
    hidden, kept, sent = head(sizes[1:], [(self_part, from_partner, near_middle, masked[1])])
    hiddens = [hidden_first, hidden]
    held = add_sums(held[0], move)
    held_last = add_sums(kept, swapped(sent, "tp", 0))
    held_last = add_sums(held_last[:2], swapped(held_last[2:], "tp", 1))
    held_last = add_sums(held_last[0], swapped(held_last[1], "tp", 2))

    def finished(held):
        held = held.astype(jnp.float32)
        inverse = lax.rsqrt((held[entries] + held[entries + EXTRA // 2]) / (8 * width) + EPS)
        logits = held[:entries] * inverse[None, :]
        top = jnp.max(logits, axis=0)
        return logits, jnp.stack([top, jnp.sum(jnp.exp(logits - top[None, :]), axis=0)])

    logits, pairs = finished(held)
    logits_last, pairs_last = finished(held_last)
    logits = jnp.concatenate([logits, logits_last], axis=1)
    pair = jnp.concatenate([pairs, pairs_last], axis=1)
    for level in range(3):
        pair = jnp.stack(combine_pair(pair, swapped(pair, "tp", level)))
    logprob = logits - (pair[0] + jnp.log(pair[1]))[None, :]
    logprob = jnp.concatenate(
        [logprob[:, r * LANES : r * LANES + L] for r in range(requests)], axis=1
    )
    return (jnp.concatenate(hiddens, axis=0).reshape(requests * L, width), logprob.T)


def on_device(
    embeds,
    remask,
    lengths,
    mask_vec,
    attn_gain,
    w_query,
    q_bias,
    w_key,
    w_value,
    v_bias,
    w_out,
    head_gain,
    w_head,
):
    requests = lengths.shape[0]
    tokens_all = embeds.shape[0]
    masked_local = jnp.where(remask[:, None] == 1, mask_vec[None, :], embeds)
    gathered = lax.all_gather(masked_local, "tp", axis=1, tiled=True)
    normed = rms_norm(gathered, attn_gain)
    queries = (
        jnp.dot(normed, w_query, preferred_element_type=jnp.float32) + q_bias.astype(jnp.float32)
    ).astype(jnp.bfloat16)
    key_rows = jnp.dot(normed, w_key, preferred_element_type=jnp.float32).astype(jnp.bfloat16)
    value_rows = (
        jnp.dot(normed, w_value, preferred_element_type=jnp.float32) + v_bias.astype(jnp.float32)
    ).astype(jnp.bfloat16)
    tp_count = lax.axis_size("tp")
    span = max(1, tp_count // KVH)
    levels = span.bit_length() - 1
    my_index = lax.axis_index("tp")
    for level in range(levels):
        other_key, other_value = swapped((key_rows, value_rows), "tp", level)
        lower = jnp.bitwise_and(jnp.right_shift(my_index, level), 1) == 0
        key_rows = jnp.where(
            lower,
            jnp.concatenate([key_rows, other_key], axis=1),
            jnp.concatenate([other_key, key_rows], axis=1),
        )
        value_rows = jnp.where(
            lower,
            jnp.concatenate([value_rows, other_value], axis=1),
            jnp.concatenate([other_value, value_rows], axis=1),
        )
    heads_dev = queries.shape[1] // HS
    kv_count = key_rows.shape[1] // HS
    repeats = heads_dev // kv_count
    k_four = jnp.repeat(key_rows.reshape(requests, L, kv_count, HS), repeats, axis=2)
    v_four = jnp.repeat(value_rows.reshape(requests, L, kv_count, HS), repeats, axis=2)
    q_four = queries.reshape(requests, L, heads_dev, HS)
    scores = jnp.einsum(
        "rqhd,rkhd->rhqk", q_four, k_four, preferred_element_type=jnp.float32
    ) * HS ** (-0.5)
    valid = jnp.arange(L, dtype=jnp.int32)[None, :] < lengths[:, None]
    scores = jnp.where(valid[:, None, None, :], scores, jnp.float32(-1e30))
    peak = jnp.max(scores, axis=-1, keepdims=True)
    expo = jnp.exp(scores - peak)
    attn_prob = (expo / jnp.sum(expo, axis=-1, keepdims=True)).astype(jnp.bfloat16)
    context = jnp.einsum(
        "rhqk,rkhd->rqhd", attn_prob, v_four, preferred_element_type=jnp.float32
    ).astype(jnp.bfloat16)
    context = context.reshape(tokens_all, heads_dev * HS)
    portion = lax.psum_scatter(
        lax.dot_general(
            w_out, context, (((0,), (1,)), ((), ())), preferred_element_type=jnp.float32
        ).astype(jnp.bfloat16),
        "tp",
        scatter_dimension=0,
        tiled=True,
    ).astype(jnp.float32)
    hidden_local = (masked_local.astype(jnp.float32) + portion.T).astype(jnp.bfloat16)
    hidden_full = lax.all_gather(hidden_local, "tp", axis=1, tiled=True)
    normed_head = rms_norm(hidden_full, head_gain)
    logits = jnp.dot(normed_head, w_head, preferred_element_type=jnp.float32)
    local_top = jnp.max(logits, axis=-1)
    local_total = jnp.sum(jnp.exp(logits - local_top[:, None]), axis=-1)
    row_top, row_total = combined_all((local_top, local_total), "tp", combine_pair)
    log_total = row_top + jnp.log(row_total)
    return (hidden_local, logits - log_total[:, None])


def solution(mesh):
    placed = (
        P("rep", "tp"),
        P("rep"),
        P("rep"),
        P("tp"),
        P(),
        P(None, "tp"),
        P("tp"),
        P(None, "tp"),
        P(None, "tp"),
        P("tp"),
        P("tp", None),
        P(),
        P(None, "tp"),
    )
    on_line_fits = mesh.shape["tp"] == CORES * CHIPS and mesh.shape["tp"] == KVH
    return jax.shard_map(
        on_line if on_line_fits else on_device,
        mesh=mesh,
        in_specs=placed,
        out_specs=(P("rep", "tp"), P("rep", "tp")),
        check_vma=False,
    )
```

```python
import functools

import jax
import jax.numpy as jnp
from jax import lax
from jax.experimental import pallas as pl
from jax.experimental.pallas import tpu as pltpu
from jax.sharding import PartitionSpec as P

KVH = 8
HS = 128
L = 196
CORES = 2
CHIPS = 4
EXTRA = 16
LANES = 256
OUT_AFTER = False
PARTNER_EARLY = False
HEAD_LATE = True
REP_EARLY = True
SECOND_EARLY = True
FIRST_DEMAND = False
DEMAND = True
VMEM_A = 56
STAGES = 2
VMEM_B = 56
GROUPS = [(0, 2), (2, 4)]


EPS = 1e-06
NT = (((1,), (1,)), ((), ()))


def swapped(value, axis, apart):
    mask = 2**apart
    pairs = [(source, source ^ mask) for source in range(lax.axis_size(axis))]
    return lax.ppermute(value, axis, pairs)


def combined_all(x, axis, combine):
    everything = jax.tree.map(lambda part: lax.all_gather(part, axis), x)
    initial = jax.tree.map(lambda part: part[0], everything)

    def lap(k, so_far):
        return combine(so_far, jax.tree.map(lambda part: part[k], everything))

    return lax.fori_loop(1, lax.axis_size(axis), lap, initial)


def rms_norm(matrix, gain):
    wide = matrix.astype(jnp.float32)
    inverse = lax.rsqrt(jnp.mean(wide * wide, axis=-1, keepdims=True) + EPS)
    return (wide * inverse * gain.astype(jnp.float32)).astype(jnp.bfloat16)


def combine_pair(first_pair, second_pair):
    top = jnp.maximum(first_pair[0], second_pair[0])
    total = first_pair[1] * jnp.exp(first_pair[0] - top) + second_pair[1] * jnp.exp(
        second_pair[0] - top
    )
    return (top, total)


def between_chips(pairs):
    return [(CORES * a + c, CORES * b + c) for a, b in pairs for c in range(CORES)]


PARTNER = between_chips([(0, 1), (1, 0), (2, 3), (3, 2)])
MIDDLE = between_chips([(1, 2), (2, 1)])
OUTWARD = between_chips([(2, 3), (1, 0)])
INWARD = between_chips([(3, 2), (0, 1)])


def permuted(value, pairs):
    return lax.ppermute(value, "tp", pairs)


def after(value, *earlier):
    return lax.optimization_barrier((value, earlier))[0]


def attend_kernel(heads, order, length, *refs):
    shards, (gain, w_q, w_k, w_v, q_bias, v_bias, context, normed, q_rows, kv_rows, sems) = refs[:8], refs[8:]
    width = shards[0].shape[1]
    group, count = context.shape[:2]
    copies = []
    for k in range(8):
        rows = pl.ds(pl.multiple_of(order[k] * width, width), width)
        here = slice(k * width, (k + 1) * width)
        copies.append(
            (
                pltpu.make_async_copy(w_q.at[rows, :], q_rows.at[here, :], sems.at[0, k]),
                pltpu.make_async_copy(w_k.at[rows, :], kv_rows.at[here, :HS], sems.at[1, k]),
                pltpu.make_async_copy(w_v.at[rows, :], kv_rows.at[here, HS:], sems.at[2, k]),
            )
        )
        for copy in copies[-1]:
            copy.start()
    total = None
    for k in range(8):
        wide = shards[k][...].astype(jnp.float32)
        part = jnp.sum(wide * wide, axis=1, keepdims=True)
        total = part if total is None else total + part
    inverse = lax.rsqrt(total / (8 * width) + EPS)
    for k in range(8):
        scaled = shards[k][...].astype(jnp.float32) * inverse * gain[pl.ds(order[k], 1), :]
        normed[:, k * width : (k + 1) * width] = scaled.astype(jnp.bfloat16)
    q_sum = kv_sum = None
    each = 8 // STAGES
    for stage in range(STAGES):
        for k in range(stage * each, (stage + 1) * each):
            for copy in copies[k]:
                copy.wait()
        rows = slice(stage * each * width, (stage + 1) * each * width)
        q_part = jnp.dot(normed[:, rows], q_rows[rows, :], preferred_element_type=jnp.float32)
        kv_part = jnp.dot(normed[:, rows], kv_rows[rows, :], preferred_element_type=jnp.float32)
        q_sum = q_part if q_sum is None else q_sum + q_part
        kv_sum = kv_part if kv_sum is None else kv_sum + kv_part
    q_sum += q_bias[...]
    for g in range(group):
        here = slice(g * count, (g + 1) * count)
        queries = q_sum[here].astype(jnp.bfloat16)
        keys = kv_sum[here, :HS].astype(jnp.bfloat16)
        values = (kv_sum[here, HS:] + v_bias[...]).astype(jnp.bfloat16)
        valid = lax.broadcasted_iota(jnp.int32, (1, count), 1) < length[g]
        done = []
        for h in range(heads):
            scores = lax.dot_general(
                queries[:, h * HS : (h + 1) * HS], keys, NT, preferred_element_type=jnp.float32
            )
            scores = jnp.where(valid, scores, jnp.float32(-1e30))
            expo = jnp.exp((scores - jnp.max(scores, axis=1, keepdims=True)) * HS ** (-0.5))
            share = 1.0 / jnp.sum(expo, axis=1, keepdims=True)
            mixed = jnp.dot(expo.astype(jnp.bfloat16), values, preferred_element_type=jnp.float32)
            done.append((mixed * share).astype(jnp.bfloat16))
        for h in range(heads):
            context[g, :, h * HS : (h + 1) * HS] = done[h]


def out_kernel(chips, blocks, own, other, w_own, w_other, *refs):
    targets, (own_rows, other_rows, own_sems, other_sems) = refs[:-4], refs[-4:]
    group, _, width = targets[0].shape
    copies = []
    for k in range(len(targets)):
        here = pl.ds(pl.multiple_of(blocks[k] * width, width), width)
        there = pl.ds(pl.multiple_of(chips[k] * width, width), width)
        copies.append(
            (
                pltpu.make_async_copy(w_own.at[:, here], own_rows.at[k], own_sems.at[k]),
                pltpu.make_async_copy(w_other.at[:, there], other_rows.at[k], other_sems.at[k]),
            )
        )
        for copy in copies[-1]:
            copy.start()
    for k in range(len(targets)):
        for copy in copies[k]:
            copy.wait()
        for g in range(group):
            part = jnp.dot(own[g], own_rows[k], preferred_element_type=jnp.float32)
            part += jnp.dot(other[g], other_rows[k], preferred_element_type=jnp.float32)
            targets[k][g] = part.astype(jnp.bfloat16)


def head_kernel(groups, *refs):
    chunks, refs = refs[: 4 * len(groups)], refs[4 * len(groups) :]
    gain, w_rows = refs[:2]
    hiddens, (keep, send) = refs[2:-2], refs[-2:]
    entries = w_rows.shape[0] // 8
    place = 0
    for i, group in enumerate(groups):
        kept, partner, middle, masked = chunks[4 * i : 4 * i + 4]
        for g in range(group):
            wide = lambda ref: ref[g].astype(jnp.float32)
            summed = wide(kept) + (wide(partner) + wide(middle))
            count = summed.shape[0]
            rows = masked[...].astype(jnp.float32)[g * count : (g + 1) * count]
            rounded = (rows + summed).astype(jnp.bfloat16)
            hiddens[i][g] = rounded
            value = rounded.astype(jnp.float32)
            scaled = (value * gain[...]).astype(jnp.bfloat16)
            logits = lax.dot_general(w_rows[...], scaled, NT, preferred_element_type=jnp.float32)
            ones = jnp.ones((EXTRA // 2, value.shape[1]), jnp.float32)
            squares = lax.dot_general(
                ones, value * value, NT, preferred_element_type=jnp.float32, precision=lax.Precision.HIGHEST
            )
            coarse = squares.astype(jnp.bfloat16)
            fine = (squares - coarse.astype(jnp.float32)).astype(jnp.bfloat16)
            both = jnp.concatenate([coarse, fine], axis=0)
            lanes = slice(place * LANES, place * LANES + value.shape[0])
            place += 1
            for row, k in enumerate((0, 4, 2, 6)):
                for target, block in ((keep, k), (send, k + 1)):
                    part = logits[block * entries : (block + 1) * entries]
                    target[row, 0:entries, lanes] = part.astype(jnp.bfloat16)
                    target[row, entries : entries + EXTRA, lanes] = both


def whole(space=pltpu.VMEM):
    return pl.BlockSpec(memory_space=space)


def head_steps(w_head, index):
    turned = w_head.T
    entries = turned.shape[0]
    width = turned.shape[1] // 8
    parts = lax.axis_size("rep")
    rep = lax.axis_index("rep")
    shared = parts & (parts - 1) == 0 and entries % (16 * parts) == 0
    if shared:
        share = entries // parts
        turned = lax.dynamic_slice_in_dim(turned, rep * share, share, axis=0)
    blocks = jnp.stack(
        [
            lax.dynamic_slice_in_dim(turned, jnp.bitwise_xor(index, k) * width, width, axis=1)
            for k in range(8)
        ]
    )
    for level in range(3):
        bit = 1 << level
        stay = [k for k in range(8) if not k & bit]
        move = [k for k in range(8) if k & bit]
        got = yield jnp.stack([blocks[k] for k in move]), "tp", level
        merged = [None] * 8
        for place, k in enumerate(stay):
            merged[k] = blocks[k]
        for place, k in enumerate(move):
            merged[k] = got[place]
        blocks = jnp.stack(merged)
    if shared:
        for level in range(parts.bit_length() - 1):
            got = yield blocks, "rep", level
            lower = jnp.bitwise_and(jnp.right_shift(rep, level), 1) == 0
            blocks = jnp.concatenate(
                [jnp.where(lower, blocks, got), jnp.where(lower, got, blocks)], axis=1
            )
    yield blocks.reshape(8 * entries, width), None, None


def on_line(
    embeds,
    remask,
    lengths,
    mask_vec,
    attn_gain,
    w_query,
    q_bias,
    w_key,
    w_value,
    v_bias,
    w_out,
    head_gain,
    w_head,
):
    requests = lengths.shape[0]
    width = embeds.shape[1]
    heads = w_query.shape[1] // HS
    entries = w_head.shape[1]
    index = lax.axis_index("tp")
    chip, core = index // CORES, index % CORES
    first_half = chip < 2
    line = jnp.stack(
        [chip, jnp.bitwise_xor(chip, 1), jnp.where(first_half, 2, 1), jnp.where(first_half, 3, 0)]
    ).astype(jnp.int32)
    places = jnp.concatenate([line * CORES + core, line * CORES + (1 - core)])
    masked = []
    for first, end in GROUPS:
        rows = slice(first * L, end * L)
        masked.append(jnp.where(remask[rows, None] == 1, mask_vec[None, :], embeds[rows]))
        embeds = after(embeds, masked[0])
    sizes = [end - first for first, end in GROUPS]

    def of_core(matrix, wanted):
        return jnp.concatenate(
            [
                lax.dynamic_slice_in_dim(matrix, (CORES * z + wanted) * width, width, axis=1)
                for z in range(CHIPS)
            ],
            axis=1,
        )

    gain = attn_gain.astype(jnp.float32).reshape(8, width)
    q_row = q_bias.astype(jnp.float32)[None, :]
    v_row = v_bias.astype(jnp.float32)[None, :]
    gain_local = lax.dynamic_slice_in_dim(head_gain, index * width, width).astype(jnp.float32)[None, :]

    steps = head_steps(w_head, index)

    def travelled(value, axis, level):
        return value if axis is None else swapped(value, axis, level)

    def next_step(step, arrived):
        return step if step[1] is None else steps.send(arrived)

    def attend(i):
        first, end = GROUPS[i]
        return pl.pallas_call(
            functools.partial(attend_kernel, heads),
            out_shape=jax.ShapeDtypeStruct((sizes[i], L, heads * HS), jnp.bfloat16),
            in_specs=[whole(pltpu.SMEM)] * 2 + [whole()] * 9 + [whole(pl.ANY)] * 3 + [whole()] * 2,
            out_specs=whole(),
            scratch_shapes=[
                pltpu.VMEM((sizes[i] * L, 8 * width), jnp.bfloat16),
                pltpu.VMEM((8 * width, heads * HS), jnp.bfloat16),
                pltpu.VMEM((8 * width, 2 * HS), jnp.bfloat16),
                pltpu.SemaphoreType.DMA((3, 8)),
            ],
            compiler_params=pltpu.CompilerParams(vmem_limit_bytes=VMEM_A * 2**20),
            cost_estimate=pl.CostEstimate(
                flops=sizes[i] * 2 * L * width * 8 * (heads * HS + 2 * HS),
                bytes_accessed=sizes[i] * 12 * 2**20,
                transcendentals=sizes[i] * heads * L * L,
            ),
        )(places, lengths[first:end], *shards[i], gain, w_query, w_key, w_value, q_row, v_row)

    def out(size, wanted, context, other):
        chips, blocks = wanted
        count = chips.shape[0]
        return pl.pallas_call(
            out_kernel,
            out_shape=[jax.ShapeDtypeStruct((size, L, width), jnp.bfloat16)] * count,
            in_specs=[whole(pltpu.SMEM)] * 2 + [whole()] * 2 + [whole(pl.ANY)] * 2,
            out_specs=[whole()] * count,
            scratch_shapes=[
                pltpu.VMEM((count, heads * HS, width), jnp.bfloat16),
                pltpu.VMEM((count, heads * HS, width), jnp.bfloat16),
                pltpu.SemaphoreType.DMA((count,)),
                pltpu.SemaphoreType.DMA((count,)),
            ],
            compiler_params=pltpu.CompilerParams(vmem_limit_bytes=VMEM_B * 2**20),
            cost_estimate=pl.CostEstimate(
                flops=size * 2 * L * width * 2 * count * heads * HS,
                bytes_accessed=size * 4 * count * 2**20,
                transcendentals=0,
            ),
        )(chips, blocks, context, other, w_out, w_other)

    def head(groups, chunks):
        count = sum(groups)
        return pl.pallas_call(
            functools.partial(head_kernel, groups),
            out_shape=[jax.ShapeDtypeStruct((size, L, width), jnp.bfloat16) for size in groups]
            + [jax.ShapeDtypeStruct((4, entries + EXTRA, count * LANES), jnp.bfloat16)] * 2,
            in_specs=[whole()] * (4 * len(groups) + 2),
            out_specs=[whole()] * (len(groups) + 2),
            compiler_params=pltpu.CompilerParams(vmem_limit_bytes=32 * 2**20),
            cost_estimate=pl.CostEstimate(
                flops=count * 2 * L * width * 8 * entries, bytes_accessed=count * 3 * 2**20, transcendentals=0
            ),
        )(*[value for chunk in chunks for value in chunk], gain_local, w_rows)

    add = lambda *terms: sum(term.astype(jnp.float32) for term in terms).astype(jnp.bfloat16)
    own, inward, middle, partner = ({} for _ in range(4))

    def advance_middle(i, *earlier):
        value = add(own[i][2], after(inward[i], *earlier))
        middle[i] = permuted(value, MIDDLE)
        return value

    def advance_partner(i, *earlier):
        value = add(own[i][1], after(middle[i][0], *earlier))
        partner[i] = permuted(value, PARTNER)
        return value

    def add_sums(kept, got):
        total = kept.astype(jnp.float32) + got.astype(jnp.float32)
        logits, coarse, fine = jnp.split(total, [entries, entries + EXTRA // 2], axis=-2)
        squares = coarse + fine
        coarse = squares.astype(jnp.bfloat16)
        fine = (squares - coarse.astype(jnp.float32)).astype(jnp.bfloat16)
        return jnp.concatenate([logits.astype(jnp.bfloat16), coarse, fine], axis=-2)

    def both_cores(*mine):
        return [*mine, *(swapped(shard, "tp", 0) for shard in mine)]

    tables = [(line[here], places[:4][here]) for here in (slice(0, 4), slice(3, 4), slice(0, 3))]
    own = masked[0]
    partner, middle = permuted(own, PARTNER), permuted(own, MIDDLE)
    step = next(steps)
    moved = travelled(*step)
    theirs = of_core(w_out, 1 - core)
    partner, middle, moved, theirs = lax.optimization_barrier((partner, middle, moved, theirs))
    far_middle, near_out = permuted(partner, MIDDLE), permuted(middle, OUTWARD)
    step = next_step(step, moved)
    moved = travelled(*step)
    far_middle, near_out, moved, ready = lax.optimization_barrier(
        (far_middle, near_out, moved, (places, line, lengths, gain, q_row, v_row, gain_local, tables))
    )
    places, line, lengths, gain, q_row, v_row, gain_local, tables = ready
    far_out = permuted(far_middle, OUTWARD)
    own = after(masked[1], partner)
    next_partner = permuted(own, PARTNER)
    next_middle = permuted(after(own, far_middle), MIDDLE)
    step = next_step(step, moved)
    if SECOND_EARLY:
        far_out, next_middle, next_partner = lax.optimization_barrier((far_out, next_middle, next_partner))
    else:
        far_out, next_middle = lax.optimization_barrier((far_out, next_middle))
    w_other = swapped(theirs, "tp", 0)
    shards = [both_cores(masked[0], partner, middle + near_out, far_middle + far_out)]

    partner, middle = next_partner, next_middle
    far_middle, near_out = permuted(partner, MIDDLE), permuted(middle, OUTWARD)
    shards[0] = after(shards[0], partner, middle)
    context = attend(0)
    other = after(swapped(context, "tp", 0), far_middle, near_out)
    self_part, partner_part, near, far = out(sizes[0], tables[0], context, other)
    far_out = permuted(after(far_middle, context), OUTWARD)
    far_out, near = lax.optimization_barrier((far_out, near))
    far_in, near_in = permuted(far, INWARD), permuted(near, INWARD)
    moved = travelled(after(step[0], far_middle), *step[1:])
    shards.append(both_cores(own, partner, middle + near_out, far_middle + far_out))

    shards[1] = after(shards[1], near)
    context = attend(1)
    context, far_in = lax.optimization_barrier((context, far_in))
    far = add(far, far_in)
    far_middle = permuted(far, MIDDLE)
    step = next_step(step, after(moved, context))
    moved = travelled(*step)
    other = swapped(context, "tp", 0)
    first_far, first_near, first_partner, first_self = far_middle, add(near, near_in), partner_part, self_part
    near_in_first = near_in
    (far,) = out(sizes[1], tables[1], context, other)
    far_in = permuted(far, INWARD)
    first_partner = add(first_partner, after(first_far, far))
    first_near = after(first_near, first_partner)
    first_parts = [first_self, permuted(first_partner, PARTNER), permuted(first_near, MIDDLE), masked[0]]
    step = next_step(step, moved)
    moved = travelled(*step)
    other = after(other, far, *(first_parts[1:3] if OUT_AFTER else ()))
    self_part, partner_part, near = out(sizes[1], tables[2], context, other)
    far_in = after(far_in, near, *((moved,) if REP_EARLY else ()), *((first_far, near_in_first) if DEMAND else ()))
    far = add(far, far_in)
    far_middle = permuted(far, MIDDLE)
    near_in = permuted(after(near, far), INWARD)
    while step[1] is not None:
        step = next_step(step, moved)
        moved = travelled(*step)
    w_rows = step[0]
    partner_sum = add(partner_part, after(far_middle, *(first_parts[1:3] if FIRST_DEMAND else ())))
    from_partner = permuted(partner_sum, PARTNER)
    near_middle = permuted(add(near, after(near_in, partner_sum)), MIDDLE)
    if HEAD_LATE:
        first_parts = after(first_parts, partner_sum)
    hidden_first, kept, sent = head(sizes[:1], [first_parts])
    near_middle = after(near_middle, kept)
    hidden, kept_last, sent_last = head(sizes[1:], [(self_part, from_partner, near_middle, masked[1])])
    hiddens = [hidden_first, hidden]
    kept = jnp.concatenate([kept, kept_last], axis=2)
    sent = jnp.concatenate([sent, sent_last], axis=2)
    held = add_sums(kept, swapped(sent, "tp", 0))
    held = add_sums(held[:2], swapped(held[2:], "tp", 1))
    held = add_sums(held[0], swapped(held[1], "tp", 2))

    def finished(held):
        held = held.astype(jnp.float32)
        inverse = lax.rsqrt((held[entries] + held[entries + EXTRA // 2]) / (8 * width) + EPS)
        logits = held[:entries] * inverse[None, :]
        top = jnp.max(logits, axis=0)
        return logits, jnp.stack([top, jnp.sum(jnp.exp(logits - top[None, :]), axis=0)])

    logits, pair = finished(held)
    for level in range(3):
        pair = jnp.stack(combine_pair(pair, swapped(pair, "tp", level)))
    logprob = logits - (pair[0] + jnp.log(pair[1]))[None, :]
    logprob = jnp.concatenate(
        [logprob[:, r * LANES : r * LANES + L] for r in range(requests)], axis=1
    )
    return (jnp.concatenate(hiddens, axis=0).reshape(requests * L, width), logprob.T)


def on_device(
    embeds,
    remask,
    lengths,
    mask_vec,
    attn_gain,
    w_query,
    q_bias,
    w_key,
    w_value,
    v_bias,
    w_out,
    head_gain,
    w_head,
):
    requests = lengths.shape[0]
    tokens_all = embeds.shape[0]
    masked_local = jnp.where(remask[:, None] == 1, mask_vec[None, :], embeds)
    gathered = lax.all_gather(masked_local, "tp", axis=1, tiled=True)
    normed = rms_norm(gathered, attn_gain)
    queries = (
        jnp.dot(normed, w_query, preferred_element_type=jnp.float32) + q_bias.astype(jnp.float32)
    ).astype(jnp.bfloat16)
    key_rows = jnp.dot(normed, w_key, preferred_element_type=jnp.float32).astype(jnp.bfloat16)
    value_rows = (
        jnp.dot(normed, w_value, preferred_element_type=jnp.float32) + v_bias.astype(jnp.float32)
    ).astype(jnp.bfloat16)
    tp_count = lax.axis_size("tp")
    span = max(1, tp_count // KVH)
    levels = span.bit_length() - 1
    my_index = lax.axis_index("tp")
    for level in range(levels):
        other_key, other_value = swapped((key_rows, value_rows), "tp", level)
        lower = jnp.bitwise_and(jnp.right_shift(my_index, level), 1) == 0
        key_rows = jnp.where(
            lower,
            jnp.concatenate([key_rows, other_key], axis=1),
            jnp.concatenate([other_key, key_rows], axis=1),
        )
        value_rows = jnp.where(
            lower,
            jnp.concatenate([value_rows, other_value], axis=1),
            jnp.concatenate([other_value, value_rows], axis=1),
        )
    heads_dev = queries.shape[1] // HS
    kv_count = key_rows.shape[1] // HS
    repeats = heads_dev // kv_count
    k_four = jnp.repeat(key_rows.reshape(requests, L, kv_count, HS), repeats, axis=2)
    v_four = jnp.repeat(value_rows.reshape(requests, L, kv_count, HS), repeats, axis=2)
    q_four = queries.reshape(requests, L, heads_dev, HS)
    scores = jnp.einsum(
        "rqhd,rkhd->rhqk", q_four, k_four, preferred_element_type=jnp.float32
    ) * HS ** (-0.5)
    valid = jnp.arange(L, dtype=jnp.int32)[None, :] < lengths[:, None]
    scores = jnp.where(valid[:, None, None, :], scores, jnp.float32(-1e30))
    peak = jnp.max(scores, axis=-1, keepdims=True)
    expo = jnp.exp(scores - peak)
    attn_prob = (expo / jnp.sum(expo, axis=-1, keepdims=True)).astype(jnp.bfloat16)
    context = jnp.einsum(
        "rhqk,rkhd->rqhd", attn_prob, v_four, preferred_element_type=jnp.float32
    ).astype(jnp.bfloat16)
    context = context.reshape(tokens_all, heads_dev * HS)
    portion = lax.psum_scatter(
        lax.dot_general(
            w_out, context, (((0,), (1,)), ((), ())), preferred_element_type=jnp.float32
        ).astype(jnp.bfloat16),
        "tp",
        scatter_dimension=0,
        tiled=True,
    ).astype(jnp.float32)
    hidden_local = (masked_local.astype(jnp.float32) + portion.T).astype(jnp.bfloat16)
    hidden_full = lax.all_gather(hidden_local, "tp", axis=1, tiled=True)
    normed_head = rms_norm(hidden_full, head_gain)
    logits = jnp.dot(normed_head, w_head, preferred_element_type=jnp.float32)
    local_top = jnp.max(logits, axis=-1)
    local_total = jnp.sum(jnp.exp(logits - local_top[:, None]), axis=-1)
    row_top, row_total = combined_all((local_top, local_total), "tp", combine_pair)
    log_total = row_top + jnp.log(row_total)
    return (hidden_local, logits - log_total[:, None])


def solution(mesh):
    placed = (
        P("rep", "tp"),
        P("rep"),
        P("rep"),
        P("tp"),
        P(),
        P(None, "tp"),
        P("tp"),
        P(None, "tp"),
        P(None, "tp"),
        P("tp"),
        P("tp", None),
        P(),
        P(None, "tp"),
    )
    on_line_fits = mesh.shape["tp"] == CORES * CHIPS and mesh.shape["tp"] == KVH
    return jax.shard_map(
        on_line if on_line_fits else on_device,
        mesh=mesh,
        in_specs=placed,
        out_specs=(P("rep", "tp"), P("rep", "tp")),
        check_vma=False,
    )
```

```python
import functools

import jax
import jax.numpy as jnp
from jax import lax
from jax.experimental import pallas as pl
from jax.experimental.pallas import tpu as pltpu
from jax.sharding import PartitionSpec as P

KVH = 8
HS = 128
L = 196
CORES = 2
CHIPS = 4
EXTRA = 16
LANES = 256
OUT_AFTER = False
PARTNER_EARLY = False
HEAD_LATE = True
REP_EARLY = True
SECOND_EARLY = True
FIRST_DEMAND = False
DEMAND = True
VMEM_A = 56
STAGES = 4
VMEM_B = 56
GROUPS = [(0, 2), (2, 4)]


EPS = 1e-06
NT = (((1,), (1,)), ((), ()))


def swapped(value, axis, apart):
    mask = 2**apart
    pairs = [(source, source ^ mask) for source in range(lax.axis_size(axis))]
    return lax.ppermute(value, axis, pairs)


def combined_all(x, axis, combine):
    everything = jax.tree.map(lambda part: lax.all_gather(part, axis), x)
    initial = jax.tree.map(lambda part: part[0], everything)

    def lap(k, so_far):
        return combine(so_far, jax.tree.map(lambda part: part[k], everything))

    return lax.fori_loop(1, lax.axis_size(axis), lap, initial)


def rms_norm(matrix, gain):
    wide = matrix.astype(jnp.float32)
    inverse = lax.rsqrt(jnp.mean(wide * wide, axis=-1, keepdims=True) + EPS)
    return (wide * inverse * gain.astype(jnp.float32)).astype(jnp.bfloat16)


def combine_pair(first_pair, second_pair):
    top = jnp.maximum(first_pair[0], second_pair[0])
    total = first_pair[1] * jnp.exp(first_pair[0] - top) + second_pair[1] * jnp.exp(
        second_pair[0] - top
    )
    return (top, total)


def between_chips(pairs):
    return [(CORES * a + c, CORES * b + c) for a, b in pairs for c in range(CORES)]


PARTNER = between_chips([(0, 1), (1, 0), (2, 3), (3, 2)])
MIDDLE = between_chips([(1, 2), (2, 1)])
OUTWARD = between_chips([(2, 3), (1, 0)])
INWARD = between_chips([(3, 2), (0, 1)])


def permuted(value, pairs):
    return lax.ppermute(value, "tp", pairs)


def after(value, *earlier):
    return lax.optimization_barrier((value, earlier))[0]


def attend_kernel(heads, order, length, *refs):
    shards, (gain, w_q, w_k, w_v, q_bias, v_bias, context, normed, q_rows, kv_rows, sems) = refs[:8], refs[8:]
    width = shards[0].shape[1]
    group, count = context.shape[:2]
    copies = []
    for k in range(8):
        rows = pl.ds(pl.multiple_of(order[k] * width, width), width)
        here = slice(k * width, (k + 1) * width)
        copies.append(
            (
                pltpu.make_async_copy(w_q.at[rows, :], q_rows.at[here, :], sems.at[0, k]),
                pltpu.make_async_copy(w_k.at[rows, :], kv_rows.at[here, :HS], sems.at[1, k]),
                pltpu.make_async_copy(w_v.at[rows, :], kv_rows.at[here, HS:], sems.at[2, k]),
            )
        )
        for copy in copies[-1]:
            copy.start()
    total = None
    for k in range(8):
        wide = shards[k][...].astype(jnp.float32)
        part = jnp.sum(wide * wide, axis=1, keepdims=True)
        total = part if total is None else total + part
    inverse = lax.rsqrt(total / (8 * width) + EPS)
    for k in range(8):
        scaled = shards[k][...].astype(jnp.float32) * inverse * gain[pl.ds(order[k], 1), :]
        normed[:, k * width : (k + 1) * width] = scaled.astype(jnp.bfloat16)
    q_sum = kv_sum = None
    each = 8 // STAGES
    for stage in range(STAGES):
        for k in range(stage * each, (stage + 1) * each):
            for copy in copies[k]:
                copy.wait()
        rows = slice(stage * each * width, (stage + 1) * each * width)
        q_part = jnp.dot(normed[:, rows], q_rows[rows, :], preferred_element_type=jnp.float32)
        kv_part = jnp.dot(normed[:, rows], kv_rows[rows, :], preferred_element_type=jnp.float32)
        q_sum = q_part if q_sum is None else q_sum + q_part
        kv_sum = kv_part if kv_sum is None else kv_sum + kv_part
    q_sum += q_bias[...]
    for g in range(group):
        here = slice(g * count, (g + 1) * count)
        queries = q_sum[here].astype(jnp.bfloat16)
        keys = kv_sum[here, :HS].astype(jnp.bfloat16)
        values = (kv_sum[here, HS:] + v_bias[...]).astype(jnp.bfloat16)
        valid = lax.broadcasted_iota(jnp.int32, (1, count), 1) < length[g]
        done = []
        for h in range(heads):
            scores = lax.dot_general(
                queries[:, h * HS : (h + 1) * HS], keys, NT, preferred_element_type=jnp.float32
            )
            scores = jnp.where(valid, scores, jnp.float32(-1e30))
            expo = jnp.exp((scores - jnp.max(scores, axis=1, keepdims=True)) * HS ** (-0.5))
            share = 1.0 / jnp.sum(expo, axis=1, keepdims=True)
            mixed = jnp.dot(expo.astype(jnp.bfloat16), values, preferred_element_type=jnp.float32)
            done.append((mixed * share).astype(jnp.bfloat16))
        for h in range(heads):
            context[g, :, h * HS : (h + 1) * HS] = done[h]


def out_kernel(chips, blocks, own, other, w_own, w_other, *refs):
    targets, (own_rows, other_rows, own_sems, other_sems) = refs[:-4], refs[-4:]
    group, _, width = targets[0].shape
    copies = []
    for k in range(len(targets)):
        here = pl.ds(pl.multiple_of(blocks[k] * width, width), width)
        there = pl.ds(pl.multiple_of(chips[k] * width, width), width)
        copies.append(
            (
                pltpu.make_async_copy(w_own.at[:, here], own_rows.at[k], own_sems.at[k]),
                pltpu.make_async_copy(w_other.at[:, there], other_rows.at[k], other_sems.at[k]),
            )
        )
        for copy in copies[-1]:
            copy.start()
    for k in range(len(targets)):
        for copy in copies[k]:
            copy.wait()
        for g in range(group):
            part = jnp.dot(own[g], own_rows[k], preferred_element_type=jnp.float32)
            part += jnp.dot(other[g], other_rows[k], preferred_element_type=jnp.float32)
            targets[k][g] = part.astype(jnp.bfloat16)


def head_kernel(groups, *refs):
    chunks, refs = refs[: 4 * len(groups)], refs[4 * len(groups) :]
    gain, w_rows = refs[:2]
    hiddens, (keep, send) = refs[2:-2], refs[-2:]
    entries = w_rows.shape[0] // 8
    place = 0
    for i, group in enumerate(groups):
        kept, partner, middle, masked = chunks[4 * i : 4 * i + 4]
        for g in range(group):
            wide = lambda ref: ref[g].astype(jnp.float32)
            summed = wide(kept) + (wide(partner) + wide(middle))
            count = summed.shape[0]
            rows = masked[...].astype(jnp.float32)[g * count : (g + 1) * count]
            rounded = (rows + summed).astype(jnp.bfloat16)
            hiddens[i][g] = rounded
            value = rounded.astype(jnp.float32)
            scaled = (value * gain[...]).astype(jnp.bfloat16)
            logits = lax.dot_general(w_rows[...], scaled, NT, preferred_element_type=jnp.float32)
            ones = jnp.ones((EXTRA // 2, value.shape[1]), jnp.float32)
            squares = lax.dot_general(
                ones, value * value, NT, preferred_element_type=jnp.float32, precision=lax.Precision.HIGHEST
            )
            coarse = squares.astype(jnp.bfloat16)
            fine = (squares - coarse.astype(jnp.float32)).astype(jnp.bfloat16)
            both = jnp.concatenate([coarse, fine], axis=0)
            lanes = slice(place * LANES, place * LANES + value.shape[0])
            place += 1
            for row, k in enumerate((0, 4, 2, 6)):
                for target, block in ((keep, k), (send, k + 1)):
                    part = logits[block * entries : (block + 1) * entries]
                    target[row, 0:entries, lanes] = part.astype(jnp.bfloat16)
                    target[row, entries : entries + EXTRA, lanes] = both


def whole(space=pltpu.VMEM):
    return pl.BlockSpec(memory_space=space)


def head_steps(w_head, index):
    turned = w_head.T
    entries = turned.shape[0]
    width = turned.shape[1] // 8
    parts = lax.axis_size("rep")
    rep = lax.axis_index("rep")
    shared = parts & (parts - 1) == 0 and entries % (16 * parts) == 0
    if shared:
        share = entries // parts
        turned = lax.dynamic_slice_in_dim(turned, rep * share, share, axis=0)
    blocks = jnp.stack(
        [
            lax.dynamic_slice_in_dim(turned, jnp.bitwise_xor(index, k) * width, width, axis=1)
            for k in range(8)
        ]
    )
    for level in range(3):
        bit = 1 << level
        stay = [k for k in range(8) if not k & bit]
        move = [k for k in range(8) if k & bit]
        got = yield jnp.stack([blocks[k] for k in move]), "tp", level
        merged = [None] * 8
        for place, k in enumerate(stay):
            merged[k] = blocks[k]
        for place, k in enumerate(move):
            merged[k] = got[place]
        blocks = jnp.stack(merged)
    if shared:
        for level in range(parts.bit_length() - 1):
            got = yield blocks, "rep", level
            lower = jnp.bitwise_and(jnp.right_shift(rep, level), 1) == 0
            blocks = jnp.concatenate(
                [jnp.where(lower, blocks, got), jnp.where(lower, got, blocks)], axis=1
            )
    yield blocks.reshape(8 * entries, width), None, None


def on_line(
    embeds,
    remask,
    lengths,
    mask_vec,
    attn_gain,
    w_query,
    q_bias,
    w_key,
    w_value,
    v_bias,
    w_out,
    head_gain,
    w_head,
):
    requests = lengths.shape[0]
    width = embeds.shape[1]
    heads = w_query.shape[1] // HS
    entries = w_head.shape[1]
    index = lax.axis_index("tp")
    chip, core = index // CORES, index % CORES
    first_half = chip < 2
    line = jnp.stack(
        [chip, jnp.bitwise_xor(chip, 1), jnp.where(first_half, 2, 1), jnp.where(first_half, 3, 0)]
    ).astype(jnp.int32)
    places = jnp.concatenate([line * CORES + core, line * CORES + (1 - core)])
    masked = []
    for first, end in GROUPS:
        rows = slice(first * L, end * L)
        masked.append(jnp.where(remask[rows, None] == 1, mask_vec[None, :], embeds[rows]))
        embeds = after(embeds, masked[0])
    sizes = [end - first for first, end in GROUPS]

    def of_core(matrix, wanted):
        return jnp.concatenate(
            [
                lax.dynamic_slice_in_dim(matrix, (CORES * z + wanted) * width, width, axis=1)
                for z in range(CHIPS)
            ],
            axis=1,
        )

    gain = attn_gain.astype(jnp.float32).reshape(8, width)
    q_row = q_bias.astype(jnp.float32)[None, :]
    v_row = v_bias.astype(jnp.float32)[None, :]
    gain_local = lax.dynamic_slice_in_dim(head_gain, index * width, width).astype(jnp.float32)[None, :]

    steps = head_steps(w_head, index)

    def travelled(value, axis, level):
        return value if axis is None else swapped(value, axis, level)

    def next_step(step, arrived):
        return step if step[1] is None else steps.send(arrived)

    def attend(i):
        first, end = GROUPS[i]
        return pl.pallas_call(
            functools.partial(attend_kernel, heads),
            out_shape=jax.ShapeDtypeStruct((sizes[i], L, heads * HS), jnp.bfloat16),
            in_specs=[whole(pltpu.SMEM)] * 2 + [whole()] * 9 + [whole(pl.ANY)] * 3 + [whole()] * 2,
            out_specs=whole(),
            scratch_shapes=[
                pltpu.VMEM((sizes[i] * L, 8 * width), jnp.bfloat16),
                pltpu.VMEM((8 * width, heads * HS), jnp.bfloat16),
                pltpu.VMEM((8 * width, 2 * HS), jnp.bfloat16),
                pltpu.SemaphoreType.DMA((3, 8)),
            ],
            compiler_params=pltpu.CompilerParams(vmem_limit_bytes=VMEM_A * 2**20),
            cost_estimate=pl.CostEstimate(
                flops=sizes[i] * 2 * L * width * 8 * (heads * HS + 2 * HS),
                bytes_accessed=sizes[i] * 12 * 2**20,
                transcendentals=sizes[i] * heads * L * L,
            ),
        )(places, lengths[first:end], *shards[i], gain, w_query, w_key, w_value, q_row, v_row)

    def out(size, wanted, context, other):
        chips, blocks = wanted
        count = chips.shape[0]
        return pl.pallas_call(
            out_kernel,
            out_shape=[jax.ShapeDtypeStruct((size, L, width), jnp.bfloat16)] * count,
            in_specs=[whole(pltpu.SMEM)] * 2 + [whole()] * 2 + [whole(pl.ANY)] * 2,
            out_specs=[whole()] * count,
            scratch_shapes=[
                pltpu.VMEM((count, heads * HS, width), jnp.bfloat16),
                pltpu.VMEM((count, heads * HS, width), jnp.bfloat16),
                pltpu.SemaphoreType.DMA((count,)),
                pltpu.SemaphoreType.DMA((count,)),
            ],
            compiler_params=pltpu.CompilerParams(vmem_limit_bytes=VMEM_B * 2**20),
            cost_estimate=pl.CostEstimate(
                flops=size * 2 * L * width * 2 * count * heads * HS,
                bytes_accessed=size * 4 * count * 2**20,
                transcendentals=0,
            ),
        )(chips, blocks, context, other, w_out, w_other)

    def head(groups, chunks):
        count = sum(groups)
        return pl.pallas_call(
            functools.partial(head_kernel, groups),
            out_shape=[jax.ShapeDtypeStruct((size, L, width), jnp.bfloat16) for size in groups]
            + [jax.ShapeDtypeStruct((4, entries + EXTRA, count * LANES), jnp.bfloat16)] * 2,
            in_specs=[whole()] * (4 * len(groups) + 2),
            out_specs=[whole()] * (len(groups) + 2),
            compiler_params=pltpu.CompilerParams(vmem_limit_bytes=32 * 2**20),
            cost_estimate=pl.CostEstimate(
                flops=count * 2 * L * width * 8 * entries, bytes_accessed=count * 3 * 2**20, transcendentals=0
            ),
        )(*[value for chunk in chunks for value in chunk], gain_local, w_rows)

    add = lambda *terms: sum(term.astype(jnp.float32) for term in terms).astype(jnp.bfloat16)
    own, inward, middle, partner = ({} for _ in range(4))

    def advance_middle(i, *earlier):
        value = add(own[i][2], after(inward[i], *earlier))
        middle[i] = permuted(value, MIDDLE)
        return value

    def advance_partner(i, *earlier):
        value = add(own[i][1], after(middle[i][0], *earlier))
        partner[i] = permuted(value, PARTNER)
        return value

    def add_sums(kept, got):
        total = kept.astype(jnp.float32) + got.astype(jnp.float32)
        logits, coarse, fine = jnp.split(total, [entries, entries + EXTRA // 2], axis=-2)
        squares = coarse + fine
        coarse = squares.astype(jnp.bfloat16)
        fine = (squares - coarse.astype(jnp.float32)).astype(jnp.bfloat16)
        return jnp.concatenate([logits.astype(jnp.bfloat16), coarse, fine], axis=-2)

    def both_cores(*mine):
        return [*mine, *(swapped(shard, "tp", 0) for shard in mine)]

    tables = [(line[here], places[:4][here]) for here in (slice(0, 4), slice(3, 4), slice(0, 3))]
    own = masked[0]
    partner, middle = permuted(own, PARTNER), permuted(own, MIDDLE)
    step = next(steps)
    moved = travelled(*step)
    theirs = of_core(w_out, 1 - core)
    partner, middle, moved, theirs = lax.optimization_barrier((partner, middle, moved, theirs))
    far_middle, near_out = permuted(partner, MIDDLE), permuted(middle, OUTWARD)
    step = next_step(step, moved)
    moved = travelled(*step)
    far_middle, near_out, moved, ready = lax.optimization_barrier(
        (far_middle, near_out, moved, (places, line, lengths, gain, q_row, v_row, gain_local, tables))
    )
    places, line, lengths, gain, q_row, v_row, gain_local, tables = ready
    far_out = permuted(far_middle, OUTWARD)
    own = after(masked[1], partner)
    next_partner = permuted(own, PARTNER)
    next_middle = permuted(after(own, far_middle), MIDDLE)
    step = next_step(step, moved)
    if SECOND_EARLY:
        far_out, next_middle, next_partner = lax.optimization_barrier((far_out, next_middle, next_partner))
    else:
        far_out, next_middle = lax.optimization_barrier((far_out, next_middle))
    w_other = swapped(theirs, "tp", 0)
    shards = [both_cores(masked[0], partner, middle + near_out, far_middle + far_out)]

    partner, middle = next_partner, next_middle
    far_middle, near_out = permuted(partner, MIDDLE), permuted(middle, OUTWARD)
    shards[0] = after(shards[0], partner, middle)
    context = attend(0)
    other = after(swapped(context, "tp", 0), far_middle, near_out)
    self_part, partner_part, near, far = out(sizes[0], tables[0], context, other)
    far_out = permuted(after(far_middle, context), OUTWARD)
    far_out, near = lax.optimization_barrier((far_out, near))
    far_in, near_in = permuted(far, INWARD), permuted(near, INWARD)
    moved = travelled(after(step[0], far_middle), *step[1:])
    shards.append(both_cores(own, partner, middle + near_out, far_middle + far_out))

    shards[1] = after(shards[1], near)
    context = attend(1)
    context, far_in = lax.optimization_barrier((context, far_in))
    far = add(far, far_in)
    far_middle = permuted(far, MIDDLE)
    step = next_step(step, after(moved, context))
    moved = travelled(*step)
    other = swapped(context, "tp", 0)
    first_far, first_near, first_partner, first_self = far_middle, add(near, near_in), partner_part, self_part
    near_in_first = near_in
    (far,) = out(sizes[1], tables[1], context, other)
    far_in = permuted(far, INWARD)
    first_partner = add(first_partner, after(first_far, far))
    first_near = after(first_near, first_partner)
    first_parts = [first_self, permuted(first_partner, PARTNER), permuted(first_near, MIDDLE), masked[0]]
    step = next_step(step, moved)
    moved = travelled(*step)
    other = after(other, far, *(first_parts[1:3] if OUT_AFTER else ()))
    self_part, partner_part, near = out(sizes[1], tables[2], context, other)
    far_in = after(far_in, near, *((moved,) if REP_EARLY else ()), *((first_far, near_in_first) if DEMAND else ()))
    far = add(far, far_in)
    far_middle = permuted(far, MIDDLE)
    near_in = permuted(after(near, far), INWARD)
    while step[1] is not None:
        step = next_step(step, moved)
        moved = travelled(*step)
    w_rows = step[0]
    partner_sum = add(partner_part, after(far_middle, *(first_parts[1:3] if FIRST_DEMAND else ())))
    from_partner = permuted(partner_sum, PARTNER)
    near_middle = permuted(add(near, after(near_in, partner_sum)), MIDDLE)
    if HEAD_LATE:
        first_parts = after(first_parts, partner_sum)
    hidden_first, kept, sent = head(sizes[:1], [first_parts])
    near_middle = after(near_middle, kept)
    hidden, kept_last, sent_last = head(sizes[1:], [(self_part, from_partner, near_middle, masked[1])])
    hiddens = [hidden_first, hidden]
    kept = jnp.concatenate([kept, kept_last], axis=2)
    sent = jnp.concatenate([sent, sent_last], axis=2)
    held = add_sums(kept, swapped(sent, "tp", 0))
    held = add_sums(held[:2], swapped(held[2:], "tp", 1))
    held = add_sums(held[0], swapped(held[1], "tp", 2))

    def finished(held):
        held = held.astype(jnp.float32)
        inverse = lax.rsqrt((held[entries] + held[entries + EXTRA // 2]) / (8 * width) + EPS)
        logits = held[:entries] * inverse[None, :]
        top = jnp.max(logits, axis=0)
        return logits, jnp.stack([top, jnp.sum(jnp.exp(logits - top[None, :]), axis=0)])

    logits, pair = finished(held)
    for level in range(3):
        pair = jnp.stack(combine_pair(pair, swapped(pair, "tp", level)))
    logprob = logits - (pair[0] + jnp.log(pair[1]))[None, :]
    logprob = jnp.concatenate(
        [logprob[:, r * LANES : r * LANES + L] for r in range(requests)], axis=1
    )
    return (jnp.concatenate(hiddens, axis=0).reshape(requests * L, width), logprob.T)


def on_device(
    embeds,
    remask,
    lengths,
    mask_vec,
    attn_gain,
    w_query,
    q_bias,
    w_key,
    w_value,
    v_bias,
    w_out,
    head_gain,
    w_head,
):
    requests = lengths.shape[0]
    tokens_all = embeds.shape[0]
    masked_local = jnp.where(remask[:, None] == 1, mask_vec[None, :], embeds)
    gathered = lax.all_gather(masked_local, "tp", axis=1, tiled=True)
    normed = rms_norm(gathered, attn_gain)
    queries = (
        jnp.dot(normed, w_query, preferred_element_type=jnp.float32) + q_bias.astype(jnp.float32)
    ).astype(jnp.bfloat16)
    key_rows = jnp.dot(normed, w_key, preferred_element_type=jnp.float32).astype(jnp.bfloat16)
    value_rows = (
        jnp.dot(normed, w_value, preferred_element_type=jnp.float32) + v_bias.astype(jnp.float32)
    ).astype(jnp.bfloat16)
    tp_count = lax.axis_size("tp")
    span = max(1, tp_count // KVH)
    levels = span.bit_length() - 1
    my_index = lax.axis_index("tp")
    for level in range(levels):
        other_key, other_value = swapped((key_rows, value_rows), "tp", level)
        lower = jnp.bitwise_and(jnp.right_shift(my_index, level), 1) == 0
        key_rows = jnp.where(
            lower,
            jnp.concatenate([key_rows, other_key], axis=1),
            jnp.concatenate([other_key, key_rows], axis=1),
        )
        value_rows = jnp.where(
            lower,
            jnp.concatenate([value_rows, other_value], axis=1),
            jnp.concatenate([other_value, value_rows], axis=1),
        )
    heads_dev = queries.shape[1] // HS
    kv_count = key_rows.shape[1] // HS
    repeats = heads_dev // kv_count
    k_four = jnp.repeat(key_rows.reshape(requests, L, kv_count, HS), repeats, axis=2)
    v_four = jnp.repeat(value_rows.reshape(requests, L, kv_count, HS), repeats, axis=2)
    q_four = queries.reshape(requests, L, heads_dev, HS)
    scores = jnp.einsum(
        "rqhd,rkhd->rhqk", q_four, k_four, preferred_element_type=jnp.float32
    ) * HS ** (-0.5)
    valid = jnp.arange(L, dtype=jnp.int32)[None, :] < lengths[:, None]
    scores = jnp.where(valid[:, None, None, :], scores, jnp.float32(-1e30))
    peak = jnp.max(scores, axis=-1, keepdims=True)
    expo = jnp.exp(scores - peak)
    attn_prob = (expo / jnp.sum(expo, axis=-1, keepdims=True)).astype(jnp.bfloat16)
    context = jnp.einsum(
        "rhqk,rkhd->rqhd", attn_prob, v_four, preferred_element_type=jnp.float32
    ).astype(jnp.bfloat16)
    context = context.reshape(tokens_all, heads_dev * HS)
    portion = lax.psum_scatter(
        lax.dot_general(
            w_out, context, (((0,), (1,)), ((), ())), preferred_element_type=jnp.float32
        ).astype(jnp.bfloat16),
        "tp",
        scatter_dimension=0,
        tiled=True,
    ).astype(jnp.float32)
    hidden_local = (masked_local.astype(jnp.float32) + portion.T).astype(jnp.bfloat16)
    hidden_full = lax.all_gather(hidden_local, "tp", axis=1, tiled=True)
    normed_head = rms_norm(hidden_full, head_gain)
    logits = jnp.dot(normed_head, w_head, preferred_element_type=jnp.float32)
    local_top = jnp.max(logits, axis=-1)
    local_total = jnp.sum(jnp.exp(logits - local_top[:, None]), axis=-1)
    row_top, row_total = combined_all((local_top, local_total), "tp", combine_pair)
    log_total = row_top + jnp.log(row_total)
    return (hidden_local, logits - log_total[:, None])


def solution(mesh):
    placed = (
        P("rep", "tp"),
        P("rep"),
        P("rep"),
        P("tp"),
        P(),
        P(None, "tp"),
        P("tp"),
        P(None, "tp"),
        P(None, "tp"),
        P("tp"),
        P("tp", None),
        P(),
        P(None, "tp"),
    )
    on_line_fits = mesh.shape["tp"] == CORES * CHIPS and mesh.shape["tp"] == KVH
    return jax.shard_map(
        on_line if on_line_fits else on_device,
        mesh=mesh,
        in_specs=placed,
        out_specs=(P("rep", "tp"), P("rep", "tp")),
        check_vma=False,
    )
```

```python
import functools

import jax
import jax.numpy as jnp
from jax import lax
from jax.experimental import pallas as pl
from jax.experimental.pallas import tpu as pltpu
from jax.sharding import PartitionSpec as P

KVH = 8
HS = 128
L = 196
CORES = 2
CHIPS = 4
EXTRA = 16
LANES = 256
OUT_AFTER = False
PARTNER_EARLY = False
HEAD_LATE = True
REP_EARLY = True
SECOND_EARLY = True
FIRST_DEMAND = False
DEMAND = True
VMEM_A = 56
STAGES = 4
VMEM_B = 56
GROUPS = [(0, 2), (2, 4)]


EPS = 1e-06
NT = (((1,), (1,)), ((), ()))


def swapped(value, axis, apart):
    mask = 2**apart
    pairs = [(source, source ^ mask) for source in range(lax.axis_size(axis))]
    return lax.ppermute(value, axis, pairs)


def combined_all(x, axis, combine):
    everything = jax.tree.map(lambda part: lax.all_gather(part, axis), x)
    initial = jax.tree.map(lambda part: part[0], everything)

    def lap(k, so_far):
        return combine(so_far, jax.tree.map(lambda part: part[k], everything))

    return lax.fori_loop(1, lax.axis_size(axis), lap, initial)


def rms_norm(matrix, gain):
    wide = matrix.astype(jnp.float32)
    inverse = lax.rsqrt(jnp.mean(wide * wide, axis=-1, keepdims=True) + EPS)
    return (wide * inverse * gain.astype(jnp.float32)).astype(jnp.bfloat16)


def combine_pair(first_pair, second_pair):
    top = jnp.maximum(first_pair[0], second_pair[0])
    total = first_pair[1] * jnp.exp(first_pair[0] - top) + second_pair[1] * jnp.exp(
        second_pair[0] - top
    )
    return (top, total)


def between_chips(pairs):
    return [(CORES * a + c, CORES * b + c) for a, b in pairs for c in range(CORES)]


PARTNER = between_chips([(0, 1), (1, 0), (2, 3), (3, 2)])
MIDDLE = between_chips([(1, 2), (2, 1)])
OUTWARD = between_chips([(2, 3), (1, 0)])
INWARD = between_chips([(3, 2), (0, 1)])


def permuted(value, pairs):
    return lax.ppermute(value, "tp", pairs)


def after(value, *earlier):
    return lax.optimization_barrier((value, earlier))[0]


def attend_kernel(heads, order, length, *refs):
    shards, (gain, w_q, w_k, w_v, q_bias, v_bias, context, normed, here_rows, q_rows, kv_rows, sems) = refs[:8], refs[8:]
    width = shards[0].shape[1]
    group, count = context.shape[:2]
    loads = [
        pltpu.make_async_copy(shard, here_rows.at[k], sems.at[3, k]) for k, shard in enumerate(shards)
    ]
    for load in loads:
        load.start()
    shards = [here_rows.at[k] for k in range(8)]
    copies = []
    for k in range(8):
        rows = pl.ds(pl.multiple_of(order[k] * width, width), width)
        here = slice(k * width, (k + 1) * width)
        copies.append(
            (
                pltpu.make_async_copy(w_q.at[rows, :], q_rows.at[here, :], sems.at[0, k]),
                pltpu.make_async_copy(w_k.at[rows, :], kv_rows.at[here, :HS], sems.at[1, k]),
                pltpu.make_async_copy(w_v.at[rows, :], kv_rows.at[here, HS:], sems.at[2, k]),
            )
        )
        for copy in copies[-1]:
            copy.start()
    total = None
    for k in range(8):
        loads[k].wait()
        wide = shards[k][...].astype(jnp.float32)
        part = jnp.sum(wide * wide, axis=1, keepdims=True)
        total = part if total is None else total + part
    inverse = lax.rsqrt(total / (8 * width) + EPS)
    for k in range(8):
        scaled = shards[k][...].astype(jnp.float32) * inverse * gain[pl.ds(order[k], 1), :]
        normed[:, k * width : (k + 1) * width] = scaled.astype(jnp.bfloat16)
    q_sum = kv_sum = None
    each = 8 // STAGES
    for stage in range(STAGES):
        for k in range(stage * each, (stage + 1) * each):
            for copy in copies[k]:
                copy.wait()
        rows = slice(stage * each * width, (stage + 1) * each * width)
        q_part = jnp.dot(normed[:, rows], q_rows[rows, :], preferred_element_type=jnp.float32)
        kv_part = jnp.dot(normed[:, rows], kv_rows[rows, :], preferred_element_type=jnp.float32)
        q_sum = q_part if q_sum is None else q_sum + q_part
        kv_sum = kv_part if kv_sum is None else kv_sum + kv_part
    q_sum += q_bias[...]
    for g in range(group):
        here = slice(g * count, (g + 1) * count)
        queries = q_sum[here].astype(jnp.bfloat16)
        keys = kv_sum[here, :HS].astype(jnp.bfloat16)
        values = (kv_sum[here, HS:] + v_bias[...]).astype(jnp.bfloat16)
        valid = lax.broadcasted_iota(jnp.int32, (1, count), 1) < length[g]
        done = []
        for h in range(heads):
            scores = lax.dot_general(
                queries[:, h * HS : (h + 1) * HS], keys, NT, preferred_element_type=jnp.float32
            )
            scores = jnp.where(valid, scores, jnp.float32(-1e30))
            expo = jnp.exp((scores - jnp.max(scores, axis=1, keepdims=True)) * HS ** (-0.5))
            share = 1.0 / jnp.sum(expo, axis=1, keepdims=True)
            mixed = jnp.dot(expo.astype(jnp.bfloat16), values, preferred_element_type=jnp.float32)
            done.append((mixed * share).astype(jnp.bfloat16))
        for h in range(heads):
            context[g, :, h * HS : (h + 1) * HS] = done[h]


def out_kernel(chips, blocks, own, other, w_own, w_other, *refs):
    targets, (own_rows, other_rows, own_sems, other_sems) = refs[:-4], refs[-4:]
    group, _, width = targets[0].shape
    copies = []
    for k in range(len(targets)):
        here = pl.ds(pl.multiple_of(blocks[k] * width, width), width)
        there = pl.ds(pl.multiple_of(chips[k] * width, width), width)
        copies.append(
            (
                pltpu.make_async_copy(w_own.at[:, here], own_rows.at[k], own_sems.at[k]),
                pltpu.make_async_copy(w_other.at[:, there], other_rows.at[k], other_sems.at[k]),
            )
        )
        for copy in copies[-1]:
            copy.start()
    for k in range(len(targets)):
        for copy in copies[k]:
            copy.wait()
        for g in range(group):
            part = jnp.dot(own[g], own_rows[k], preferred_element_type=jnp.float32)
            part += jnp.dot(other[g], other_rows[k], preferred_element_type=jnp.float32)
            targets[k][g] = part.astype(jnp.bfloat16)


def head_kernel(groups, *refs):
    chunks, refs = refs[: 4 * len(groups)], refs[4 * len(groups) :]
    gain, w_rows = refs[:2]
    hiddens, (keep, send) = refs[2:-2], refs[-2:]
    entries = w_rows.shape[0] // 8
    place = 0
    for i, group in enumerate(groups):
        kept, partner, middle, masked = chunks[4 * i : 4 * i + 4]
        for g in range(group):
            wide = lambda ref: ref[g].astype(jnp.float32)
            summed = wide(kept) + (wide(partner) + wide(middle))
            count = summed.shape[0]
            rows = masked[...].astype(jnp.float32)[g * count : (g + 1) * count]
            rounded = (rows + summed).astype(jnp.bfloat16)
            hiddens[i][g] = rounded
            value = rounded.astype(jnp.float32)
            scaled = (value * gain[...]).astype(jnp.bfloat16)
            logits = lax.dot_general(w_rows[...], scaled, NT, preferred_element_type=jnp.float32)
            ones = jnp.ones((EXTRA // 2, value.shape[1]), jnp.float32)
            squares = lax.dot_general(
                ones, value * value, NT, preferred_element_type=jnp.float32, precision=lax.Precision.HIGHEST
            )
            coarse = squares.astype(jnp.bfloat16)
            fine = (squares - coarse.astype(jnp.float32)).astype(jnp.bfloat16)
            both = jnp.concatenate([coarse, fine], axis=0)
            lanes = slice(place * LANES, place * LANES + value.shape[0])
            place += 1
            for row, k in enumerate((0, 4, 2, 6)):
                for target, block in ((keep, k), (send, k + 1)):
                    part = logits[block * entries : (block + 1) * entries]
                    target[row, 0:entries, lanes] = part.astype(jnp.bfloat16)
                    target[row, entries : entries + EXTRA, lanes] = both


def whole(space=pltpu.VMEM):
    return pl.BlockSpec(memory_space=space)


def head_steps(w_head, index):
    turned = w_head.T
    entries = turned.shape[0]
    width = turned.shape[1] // 8
    parts = lax.axis_size("rep")
    rep = lax.axis_index("rep")
    shared = parts & (parts - 1) == 0 and entries % (16 * parts) == 0
    if shared:
        share = entries // parts
        turned = lax.dynamic_slice_in_dim(turned, rep * share, share, axis=0)
    blocks = jnp.stack(
        [
            lax.dynamic_slice_in_dim(turned, jnp.bitwise_xor(index, k) * width, width, axis=1)
            for k in range(8)
        ]
    )
    for level in range(3):
        bit = 1 << level
        stay = [k for k in range(8) if not k & bit]
        move = [k for k in range(8) if k & bit]
        got = yield jnp.stack([blocks[k] for k in move]), "tp", level
        merged = [None] * 8
        for place, k in enumerate(stay):
            merged[k] = blocks[k]
        for place, k in enumerate(move):
            merged[k] = got[place]
        blocks = jnp.stack(merged)
    if shared:
        for level in range(parts.bit_length() - 1):
            got = yield blocks, "rep", level
            lower = jnp.bitwise_and(jnp.right_shift(rep, level), 1) == 0
            blocks = jnp.concatenate(
                [jnp.where(lower, blocks, got), jnp.where(lower, got, blocks)], axis=1
            )
    yield blocks.reshape(8 * entries, width), None, None


def on_line(
    embeds,
    remask,
    lengths,
    mask_vec,
    attn_gain,
    w_query,
    q_bias,
    w_key,
    w_value,
    v_bias,
    w_out,
    head_gain,
    w_head,
):
    requests = lengths.shape[0]
    width = embeds.shape[1]
    heads = w_query.shape[1] // HS
    entries = w_head.shape[1]
    index = lax.axis_index("tp")
    chip, core = index // CORES, index % CORES
    first_half = chip < 2
    line = jnp.stack(
        [chip, jnp.bitwise_xor(chip, 1), jnp.where(first_half, 2, 1), jnp.where(first_half, 3, 0)]
    ).astype(jnp.int32)
    places = jnp.concatenate([line * CORES + core, line * CORES + (1 - core)])
    masked = []
    for first, end in GROUPS:
        rows = slice(first * L, end * L)
        masked.append(jnp.where(remask[rows, None] == 1, mask_vec[None, :], embeds[rows]))
        embeds = after(embeds, masked[0])
    sizes = [end - first for first, end in GROUPS]

    def of_core(matrix, wanted):
        return jnp.concatenate(
            [
                lax.dynamic_slice_in_dim(matrix, (CORES * z + wanted) * width, width, axis=1)
                for z in range(CHIPS)
            ],
            axis=1,
        )

    gain = attn_gain.astype(jnp.float32).reshape(8, width)
    q_row = q_bias.astype(jnp.float32)[None, :]
    v_row = v_bias.astype(jnp.float32)[None, :]
    gain_local = lax.dynamic_slice_in_dim(head_gain, index * width, width).astype(jnp.float32)[None, :]

    steps = head_steps(w_head, index)

    def travelled(value, axis, level):
        return value if axis is None else swapped(value, axis, level)

    def next_step(step, arrived):
        return step if step[1] is None else steps.send(arrived)

    def attend(i):
        first, end = GROUPS[i]
        return pl.pallas_call(
            functools.partial(attend_kernel, heads),
            out_shape=jax.ShapeDtypeStruct((sizes[i], L, heads * HS), jnp.bfloat16),
            in_specs=[whole(pltpu.SMEM)] * 2 + [whole(pl.ANY)] * 8 + [whole()] + [whole(pl.ANY)] * 3 + [whole()] * 2,
            out_specs=whole(),
            scratch_shapes=[
                pltpu.VMEM((sizes[i] * L, 8 * width), jnp.bfloat16),
                pltpu.VMEM((8, sizes[i] * L, width), jnp.bfloat16),
                pltpu.VMEM((8 * width, heads * HS), jnp.bfloat16),
                pltpu.VMEM((8 * width, 2 * HS), jnp.bfloat16),
                pltpu.SemaphoreType.DMA((4, 8)),
            ],
            compiler_params=pltpu.CompilerParams(vmem_limit_bytes=VMEM_A * 2**20),
            cost_estimate=pl.CostEstimate(
                flops=sizes[i] * 2 * L * width * 8 * (heads * HS + 2 * HS),
                bytes_accessed=sizes[i] * 12 * 2**20,
                transcendentals=sizes[i] * heads * L * L,
            ),
        )(places, lengths[first:end], *shards[i], gain, w_query, w_key, w_value, q_row, v_row)

    def out(size, wanted, context, other):
        chips, blocks = wanted
        count = chips.shape[0]
        return pl.pallas_call(
            out_kernel,
            out_shape=[jax.ShapeDtypeStruct((size, L, width), jnp.bfloat16)] * count,
            in_specs=[whole(pltpu.SMEM)] * 2 + [whole()] * 2 + [whole(pl.ANY)] * 2,
            out_specs=[whole()] * count,
            scratch_shapes=[
                pltpu.VMEM((count, heads * HS, width), jnp.bfloat16),
                pltpu.VMEM((count, heads * HS, width), jnp.bfloat16),
                pltpu.SemaphoreType.DMA((count,)),
                pltpu.SemaphoreType.DMA((count,)),
            ],
            compiler_params=pltpu.CompilerParams(vmem_limit_bytes=VMEM_B * 2**20),
            cost_estimate=pl.CostEstimate(
                flops=size * 2 * L * width * 2 * count * heads * HS,
                bytes_accessed=size * 4 * count * 2**20,
                transcendentals=0,
            ),
        )(chips, blocks, context, other, w_out, w_other)

    def head(groups, chunks):
        count = sum(groups)
        return pl.pallas_call(
            functools.partial(head_kernel, groups),
            out_shape=[jax.ShapeDtypeStruct((size, L, width), jnp.bfloat16) for size in groups]
            + [jax.ShapeDtypeStruct((4, entries + EXTRA, count * LANES), jnp.bfloat16)] * 2,
            in_specs=[whole()] * (4 * len(groups) + 2),
            out_specs=[whole()] * (len(groups) + 2),
            compiler_params=pltpu.CompilerParams(vmem_limit_bytes=32 * 2**20),
            cost_estimate=pl.CostEstimate(
                flops=count * 2 * L * width * 8 * entries, bytes_accessed=count * 3 * 2**20, transcendentals=0
            ),
        )(*[value for chunk in chunks for value in chunk], gain_local, w_rows)

    add = lambda *terms: sum(term.astype(jnp.float32) for term in terms).astype(jnp.bfloat16)
    own, inward, middle, partner = ({} for _ in range(4))

    def advance_middle(i, *earlier):
        value = add(own[i][2], after(inward[i], *earlier))
        middle[i] = permuted(value, MIDDLE)
        return value

    def advance_partner(i, *earlier):
        value = add(own[i][1], after(middle[i][0], *earlier))
        partner[i] = permuted(value, PARTNER)
        return value

    def add_sums(kept, got):
        total = kept.astype(jnp.float32) + got.astype(jnp.float32)
        logits, coarse, fine = jnp.split(total, [entries, entries + EXTRA // 2], axis=-2)
        squares = coarse + fine
        coarse = squares.astype(jnp.bfloat16)
        fine = (squares - coarse.astype(jnp.float32)).astype(jnp.bfloat16)
        return jnp.concatenate([logits.astype(jnp.bfloat16), coarse, fine], axis=-2)

    def both_cores(*mine):
        return [*mine, *(swapped(shard, "tp", 0) for shard in mine)]

    tables = [(line[here], places[:4][here]) for here in (slice(0, 4), slice(3, 4), slice(0, 3))]
    own = masked[0]
    partner, middle = permuted(own, PARTNER), permuted(own, MIDDLE)
    step = next(steps)
    moved = travelled(*step)
    theirs = of_core(w_out, 1 - core)
    partner, middle, moved, theirs = lax.optimization_barrier((partner, middle, moved, theirs))
    far_middle, near_out = permuted(partner, MIDDLE), permuted(middle, OUTWARD)
    step = next_step(step, moved)
    moved = travelled(*step)
    far_middle, near_out, moved, ready = lax.optimization_barrier(
        (far_middle, near_out, moved, (places, line, lengths, gain, q_row, v_row, gain_local, tables))
    )
    places, line, lengths, gain, q_row, v_row, gain_local, tables = ready
    far_out = permuted(far_middle, OUTWARD)
    own = after(masked[1], partner)
    next_partner = permuted(own, PARTNER)
    next_middle = permuted(after(own, far_middle), MIDDLE)
    step = next_step(step, moved)
    if SECOND_EARLY:
        far_out, next_middle, next_partner = lax.optimization_barrier((far_out, next_middle, next_partner))
    else:
        far_out, next_middle = lax.optimization_barrier((far_out, next_middle))
    w_other = swapped(theirs, "tp", 0)
    shards = [both_cores(masked[0], partner, middle + near_out, far_middle + far_out)]

    partner, middle = next_partner, next_middle
    far_middle, near_out = permuted(partner, MIDDLE), permuted(middle, OUTWARD)
    shards[0] = after(shards[0], partner, middle)
    context = attend(0)
    other = after(swapped(context, "tp", 0), far_middle, near_out)
    self_part, partner_part, near, far = out(sizes[0], tables[0], context, other)
    far_out = permuted(after(far_middle, context), OUTWARD)
    far_out, near = lax.optimization_barrier((far_out, near))
    far_in, near_in = permuted(far, INWARD), permuted(near, INWARD)
    moved = travelled(after(step[0], far_middle), *step[1:])
    shards.append(both_cores(own, partner, middle + near_out, far_middle + far_out))

    shards[1] = after(shards[1], near)
    context = attend(1)
    context, far_in = lax.optimization_barrier((context, far_in))
    far = add(far, far_in)
    far_middle = permuted(far, MIDDLE)
    step = next_step(step, after(moved, context))
    moved = travelled(*step)
    other = swapped(context, "tp", 0)
    first_far, first_near, first_partner, first_self = far_middle, add(near, near_in), partner_part, self_part
    near_in_first = near_in
    (far,) = out(sizes[1], tables[1], context, other)
    far_in = permuted(far, INWARD)
    first_partner = add(first_partner, after(first_far, far))
    first_near = after(first_near, first_partner)
    first_parts = [first_self, permuted(first_partner, PARTNER), permuted(first_near, MIDDLE), masked[0]]
    step = next_step(step, moved)
    moved = travelled(*step)
    other = after(other, far, *(first_parts[1:3] if OUT_AFTER else ()))
    self_part, partner_part, near = out(sizes[1], tables[2], context, other)
    far_in = after(far_in, near, *((moved,) if REP_EARLY else ()), *((first_far, near_in_first) if DEMAND else ()))
    far = add(far, far_in)
    far_middle = permuted(far, MIDDLE)
    near_in = permuted(after(near, far), INWARD)
    while step[1] is not None:
        step = next_step(step, moved)
        moved = travelled(*step)
    w_rows = step[0]
    partner_sum = add(partner_part, after(far_middle, *(first_parts[1:3] if FIRST_DEMAND else ())))
    from_partner = permuted(partner_sum, PARTNER)
    near_middle = permuted(add(near, after(near_in, partner_sum)), MIDDLE)
    if HEAD_LATE:
        first_parts = after(first_parts, partner_sum)
    hidden_first, kept, sent = head(sizes[:1], [first_parts])
    near_middle = after(near_middle, kept)
    hidden, kept_last, sent_last = head(sizes[1:], [(self_part, from_partner, near_middle, masked[1])])
    hiddens = [hidden_first, hidden]
    kept = jnp.concatenate([kept, kept_last], axis=2)
    sent = jnp.concatenate([sent, sent_last], axis=2)
    held = add_sums(kept, swapped(sent, "tp", 0))
    held = add_sums(held[:2], swapped(held[2:], "tp", 1))
    held = add_sums(held[0], swapped(held[1], "tp", 2))

    def finished(held):
        held = held.astype(jnp.float32)
        inverse = lax.rsqrt((held[entries] + held[entries + EXTRA // 2]) / (8 * width) + EPS)
        logits = held[:entries] * inverse[None, :]
        top = jnp.max(logits, axis=0)
        return logits, jnp.stack([top, jnp.sum(jnp.exp(logits - top[None, :]), axis=0)])

    logits, pair = finished(held)
    for level in range(3):
        pair = jnp.stack(combine_pair(pair, swapped(pair, "tp", level)))
    logprob = logits - (pair[0] + jnp.log(pair[1]))[None, :]
    logprob = jnp.concatenate(
        [logprob[:, r * LANES : r * LANES + L] for r in range(requests)], axis=1
    )
    return (jnp.concatenate(hiddens, axis=0).reshape(requests * L, width), logprob.T)


def on_device(
    embeds,
    remask,
    lengths,
    mask_vec,
    attn_gain,
    w_query,
    q_bias,
    w_key,
    w_value,
    v_bias,
    w_out,
    head_gain,
    w_head,
):
    requests = lengths.shape[0]
    tokens_all = embeds.shape[0]
    masked_local = jnp.where(remask[:, None] == 1, mask_vec[None, :], embeds)
    gathered = lax.all_gather(masked_local, "tp", axis=1, tiled=True)
    normed = rms_norm(gathered, attn_gain)
    queries = (
        jnp.dot(normed, w_query, preferred_element_type=jnp.float32) + q_bias.astype(jnp.float32)
    ).astype(jnp.bfloat16)
    key_rows = jnp.dot(normed, w_key, preferred_element_type=jnp.float32).astype(jnp.bfloat16)
    value_rows = (
        jnp.dot(normed, w_value, preferred_element_type=jnp.float32) + v_bias.astype(jnp.float32)
    ).astype(jnp.bfloat16)
    tp_count = lax.axis_size("tp")
    span = max(1, tp_count // KVH)
    levels = span.bit_length() - 1
    my_index = lax.axis_index("tp")
    for level in range(levels):
        other_key, other_value = swapped((key_rows, value_rows), "tp", level)
        lower = jnp.bitwise_and(jnp.right_shift(my_index, level), 1) == 0
        key_rows = jnp.where(
            lower,
            jnp.concatenate([key_rows, other_key], axis=1),
            jnp.concatenate([other_key, key_rows], axis=1),
        )
        value_rows = jnp.where(
            lower,
            jnp.concatenate([value_rows, other_value], axis=1),
            jnp.concatenate([other_value, value_rows], axis=1),
        )
    heads_dev = queries.shape[1] // HS
    kv_count = key_rows.shape[1] // HS
    repeats = heads_dev // kv_count
    k_four = jnp.repeat(key_rows.reshape(requests, L, kv_count, HS), repeats, axis=2)
    v_four = jnp.repeat(value_rows.reshape(requests, L, kv_count, HS), repeats, axis=2)
    q_four = queries.reshape(requests, L, heads_dev, HS)
    scores = jnp.einsum(
        "rqhd,rkhd->rhqk", q_four, k_four, preferred_element_type=jnp.float32
    ) * HS ** (-0.5)
    valid = jnp.arange(L, dtype=jnp.int32)[None, :] < lengths[:, None]
    scores = jnp.where(valid[:, None, None, :], scores, jnp.float32(-1e30))
    peak = jnp.max(scores, axis=-1, keepdims=True)
    expo = jnp.exp(scores - peak)
    attn_prob = (expo / jnp.sum(expo, axis=-1, keepdims=True)).astype(jnp.bfloat16)
    context = jnp.einsum(
        "rhqk,rkhd->rqhd", attn_prob, v_four, preferred_element_type=jnp.float32
    ).astype(jnp.bfloat16)
    context = context.reshape(tokens_all, heads_dev * HS)
    portion = lax.psum_scatter(
        lax.dot_general(
            w_out, context, (((0,), (1,)), ((), ())), preferred_element_type=jnp.float32
        ).astype(jnp.bfloat16),
        "tp",
        scatter_dimension=0,
        tiled=True,
    ).astype(jnp.float32)
    hidden_local = (masked_local.astype(jnp.float32) + portion.T).astype(jnp.bfloat16)
    hidden_full = lax.all_gather(hidden_local, "tp", axis=1, tiled=True)
    normed_head = rms_norm(hidden_full, head_gain)
    logits = jnp.dot(normed_head, w_head, preferred_element_type=jnp.float32)
    local_top = jnp.max(logits, axis=-1)
    local_total = jnp.sum(jnp.exp(logits - local_top[:, None]), axis=-1)
    row_top, row_total = combined_all((local_top, local_total), "tp", combine_pair)
    log_total = row_top + jnp.log(row_total)
    return (hidden_local, logits - log_total[:, None])


def solution(mesh):
    placed = (
        P("rep", "tp"),
        P("rep"),
        P("rep"),
        P("tp"),
        P(),
        P(None, "tp"),
        P("tp"),
        P(None, "tp"),
        P(None, "tp"),
        P("tp"),
        P("tp", None),
        P(),
        P(None, "tp"),
    )
    on_line_fits = mesh.shape["tp"] == CORES * CHIPS and mesh.shape["tp"] == KVH
    return jax.shard_map(
        on_line if on_line_fits else on_device,
        mesh=mesh,
        in_specs=placed,
        out_specs=(P("rep", "tp"), P("rep", "tp")),
        check_vma=False,
    )
```
